32 devices in a mesh: frag: 2 (over y), pair: 4 (over z), occ: 4 (over x, core).
Axes of the slice: x: 2, y: 2, z: 4, core: 2. Of those that a mesh axis runs over, the one named last changes fastest.
Arguments:
- quarter_integrals: bfloat16 [24, 12, 128, 128], P(('frag', 'occ'), 'pair'), parts along dimension 0, may hold values from -6 to 6
- occ_coef: bfloat16 [2560, 1536], P('frag', 'occ'), parts along dimension 0, may hold values from -0.5 to 0.5
- vir_coef: bfloat16 [2560, 4096], P('frag', 'occ'), parts along dimension 0, may hold values from -0.15625 to 0.15625
- screened_block_mask: int32 [20, 10], P('frag'), parts along dimension 0, may hold values from 0 to 1, as said below
- tile_holder_pair: int32 [20, 10], P('frag'), parts along dimension 0, may hold values from 0 to 3, as said below
- shell_size: int32 [20], P('frag'), parts along dimension 0, may hold values from 64 to 128
Outputs:
- mo_block: bfloat16 [24, 1536, 4096], P('frag', 'pair', 'occ'), parts along dimension 0
The draws below stay inside these ranges and needn't reach their ends.
There are 2 independent parts, one for each index of `frag`. The reference program is written for one: setup_inputs(seed, part) draws one part's arguments, and reference() takes and returns one part's arrays. A program takes and returns all parts, laid end to end along the dimension named above; each array names one. Nothing has to cross between parts.
Inputs may be any that keep to these rules, and one draw needn't show every extreme that they name: screened_block_mask is 1 for the shell-block pairs kept by the screening. At most 3 kept pairs have the same tile_holder_pair, and some pair index owns exactly 3. For a kept pair, tile_holder_pair is the pair index whose slots hold its tile; for other pairs it has no meaning.
All inputs are finite; a program needn't handle non-finite values.
Results may differ from the reference program's by a relative error of at most 0.0057.
Values may be sent and summed in bfloat16 or wider, within the bound.
A program may use at most 64 MiB of HBM per device.

```python
import jax
import jax.numpy as jnp
from jax import lax

BASIS_WIDTH = 128
NB = 10
PAIR_TILE_SLOTS = 3
NOCC = 1536
INTEGRAL_ROWS = 12
FRAGMENT_SLOTS = 12
NVIR = 4096
N_PAIR = 4


def tile_layout(key):
    count_key = jax.random.fold_in(key, 11)
    top_key = jax.random.fold_in(key, 12)
    order_key = jax.random.fold_in(key, 13)
    spare_key = jax.random.fold_in(key, 14)
    devices = jnp.arange(N_PAIR, dtype=jnp.int32)
    counts = jax.random.randint(count_key, (N_PAIR,), 0, PAIR_TILE_SLOTS + 1, dtype=jnp.int32)
    busiest = jax.random.randint(top_key, (), 0, N_PAIR, dtype=jnp.int32)
    counts = jnp.where(devices == busiest, PAIR_TILE_SLOTS, counts).astype(jnp.int32)
    slot_ends = jnp.cumsum(counts).astype(jnp.int32)
    tile_order = jax.random.permutation(order_key, NB * NB).astype(jnp.int32)
    position = jnp.zeros((NB * NB,), jnp.int32).at[tile_order].set(jnp.arange(NB * NB, dtype=jnp.int32))
    kept_tiles = position < slot_ends[-1]
    holder = jnp.sum((position[:, None] >= slot_ends[None, :]).astype(jnp.int32), axis=1).astype(jnp.int32)
    spare_owner = jax.random.randint(spare_key, (NB * NB,), 0, N_PAIR, dtype=jnp.int32)
    owners = jnp.where(kept_tiles, holder, spare_owner).astype(jnp.int32)
    return (kept_tiles.astype(jnp.int32).reshape(NB, NB), owners.reshape(NB, NB))


def draw_screened_block_mask(key, part):
    layout = tile_layout(key)
    return layout[0]


def draw_tile_holder_pair(key, part):
    layout = tile_layout(key)
    return layout[1]


def touch_ends(result, key, least, largest):
    shape = result.shape
    place = [jax.random.randint(jax.random.fold_in(key, axis), (), 0, shape[axis]) for axis in range(len(shape))]
    result = result.at[tuple(place)].set(least)
    longest = shape.index(max(shape))
    place[longest] = (place[longest] + 1) % shape[longest]
    return result.at[tuple(place)].set(largest)


def levels(stream_key, extent, split, smallest, largest):
    factor_of = 1.0
    for dim, shards_of in split:
        steps = jax.random.uniform(jax.random.fold_in(jax.random.fold_in(stream_key, 6), dim), (shards_of,), jnp.float32, smallest / len(split), largest / len(split))
        factor_of = factor_of * jnp.repeat(jnp.exp(steps), extent[dim] // shards_of).reshape((-1,) + (1,) * (len(extent) - 1 - dim))
    return factor_of


def gaussian(stream_key, shape, width, most, cuts=(), kind=jnp.bfloat16):
    drawn = width * jax.random.normal(stream_key, shape, jnp.float32)
    if cuts:
        drawn = drawn * levels(stream_key, shape, cuts, -0.22, 0.18)
    return jnp.clip(drawn, -most, most).astype(kind)


def setup_inputs(seed: int = 0, part: int = 0) -> dict:
    key_list = jax.random.split(jax.random.key(seed), 7)
    part_keys = jax.random.split(jax.random.fold_in(key_list[6], part), 7)
    quarter_integrals = gaussian(part_keys[0], (INTEGRAL_ROWS, FRAGMENT_SLOTS, BASIS_WIDTH, BASIS_WIDTH), 1.0, 6.0, ((0, 4), (1, 4)))
    occ_coef = gaussian(part_keys[1], (NB * BASIS_WIDTH, NOCC), BASIS_WIDTH ** -0.5, 0.5, ((1, 4),))
    vir_coef = gaussian(part_keys[2], (NB * BASIS_WIDTH, NVIR), (NB * BASIS_WIDTH) ** -0.5, 0.15625, ((1, 4),))
    screened_block_mask = draw_screened_block_mask(jax.random.fold_in(jax.random.fold_in(key_list[6], part), 71), part)
    tile_holder_pair = draw_tile_holder_pair(jax.random.fold_in(jax.random.fold_in(key_list[6], part), 71), part)
    shell_size = touch_ends(jax.random.randint(part_keys[5], (NB,), BASIS_WIDTH // 2, BASIS_WIDTH + 1), jax.random.fold_in(part_keys[5], 1), BASIS_WIDTH // 2, BASIS_WIDTH).astype(jnp.int32)
    return dict(quarter_integrals=quarter_integrals, occ_coef=occ_coef, vir_coef=vir_coef, screened_block_mask=screened_block_mask, tile_holder_pair=tile_holder_pair, shell_size=shell_size)


def slot_lookup_table(screened_block_mask, tile_holder_pair, slot_count, tile_slots):
    block_count = screened_block_mask.shape[0]
    kept_tiles = screened_block_mask.reshape(-1)
    owners = tile_holder_pair.reshape(-1)
    tile_index = jnp.arange(kept_tiles.shape[0], dtype=jnp.int32)
    earlier = (owners[:, None] == owners[None, :]) & (tile_index[None, :] < tile_index[:, None]) & (kept_tiles[None, :] == 1)
    rank_within = jnp.sum(earlier.astype(jnp.int32), axis=1).astype(jnp.int32)
    slot_of = (owners * tile_slots + rank_within).astype(jnp.int32)
    slot_index = jnp.arange(slot_count, dtype=jnp.int32)
    holding = ((slot_of[None, :] == slot_index[:, None]) & (kept_tiles[None, :] == 1)).astype(jnp.int32)
    slot_occupied_flag = jnp.sum(holding, axis=1).astype(jnp.int32)
    slot_lambda_block = jnp.sum(holding * (tile_index // block_count)[None, :], axis=1).astype(jnp.int32)
    slot_sigma_block = jnp.sum(holding * (tile_index % block_count)[None, :], axis=1).astype(jnp.int32)
    return slot_occupied_flag, slot_lambda_block, slot_sigma_block


def trim_rows(coefficients, shell_size, slot_width):
    inside = jnp.arange(slot_width, dtype=jnp.int32)[None, :] < shell_size[:, None]
    return jnp.where(inside.reshape(-1)[:, None], coefficients, jnp.zeros((), coefficients.dtype))


def reference(quarter_integrals, occ_coef, vir_coef, screened_block_mask, tile_holder_pair, shell_size):
    block_count = screened_block_mask.shape[0]
    slot_width = quarter_integrals.shape[3]
    slot_occupied_flag, slot_lambda_block, slot_sigma_block = slot_lookup_table(screened_block_mask, tile_holder_pair, FRAGMENT_SLOTS, PAIR_TILE_SLOTS)
    occ_used = trim_rows(occ_coef, shell_size, slot_width)
    vir_used = trim_rows(vir_coef, shell_size, slot_width)
    occ_blocks = occ_used.reshape(block_count, slot_width, NOCC)

    def add_tile(running, slot_item):
        tile_block, used_one, lam_one, sig_one = slot_item
        panel_rows = lax.dynamic_index_in_dim(occ_blocks, lam_one, 0, keepdims=False)
        tile_part = jnp.einsum("rls,lj->rjs", tile_block.astype(jnp.float32), panel_rows.astype(jnp.float32))
        tile_part = lax.optimization_barrier(tile_part.astype(jnp.bfloat16)).astype(jnp.float32)
        tile_part = tile_part * (used_one > 0).astype(jnp.float32)
        where_at = (sig_one * slot_width).astype(jnp.int32)
        current = lax.dynamic_slice_in_dim(running, where_at, slot_width, 2)
        return lax.dynamic_update_slice_in_dim(running, current + tile_part, where_at, 2), None

    start_total = jnp.zeros((quarter_integrals.shape[0], NOCC, block_count * slot_width), jnp.float32)
    summed, unused = lax.scan(add_tile, start_total, (jnp.moveaxis(quarter_integrals, 1, 0), slot_occupied_flag, slot_lambda_block, slot_sigma_block))
    half_mo = summed.astype(jnp.bfloat16)

    def project_row(row_block):
        return jnp.dot(row_block, vir_used, preferred_element_type=jnp.float32).astype(jnp.bfloat16)

    return lax.map(project_row, half_mo)
```

```python
import functools

import jax
import jax.numpy as jnp
from jax import lax
from jax.experimental import pallas as pl
from jax.experimental.pallas import tpu as pltpu
from jax.sharding import PartitionSpec as P


def slot_lookup_table(screened_block_mask, tile_holder_pair, slot_count, tile_slots):
    block_count = screened_block_mask.shape[0]
    kept_tiles = screened_block_mask.reshape(-1)
    owners = tile_holder_pair.reshape(-1)
    tile_index = jnp.arange(kept_tiles.shape[0], dtype=jnp.int32)
    earlier = (
        (owners[:, None] == owners[None, :])
        & (tile_index[None, :] < tile_index[:, None])
        & (kept_tiles[None, :] == 1)
    )
    rank_within = jnp.sum(earlier.astype(jnp.int32), axis=1)
    slot_of = owners * tile_slots + rank_within
    slot_index = jnp.arange(slot_count, dtype=jnp.int32)
    holding = ((slot_of[None, :] == slot_index[:, None]) & (kept_tiles[None, :] == 1)).astype(
        jnp.int32
    )
    slot_occupied_flag = jnp.sum(holding, axis=1)
    slot_lambda_block = jnp.sum(holding * (tile_index // block_count)[None, :], axis=1)
    slot_sigma_block = jnp.sum(holding * (tile_index % block_count)[None, :], axis=1)
    return (slot_occupied_flag, slot_lambda_block, slot_sigma_block)


def trim_rows(coefficients, shell_size, slot_width):
    inside = jnp.arange(slot_width, dtype=jnp.int32)[None, :] < shell_size[:, None]
    return jnp.where(inside.reshape(-1)[:, None], coefficients, jnp.zeros((), coefficients.dtype))


def spread_tiles(placing, tile_parts):
    spread = jnp.einsum("kn,krjs->rjns", placing, tile_parts, preferred_element_type=jnp.float32)
    return spread.reshape(spread.shape[0], spread.shape[1], -1)


def send_tiles(
    quarter_integrals, occ_coef, vir_coef, screened_block_mask, tile_holder_pair, shell_size
):
    block_count = screened_block_mask.shape[0]
    slot_width = quarter_integrals.shape[3]
    tile_slots = quarter_integrals.shape[1]
    pair_count = lax.axis_size("pair")
    pair_index = lax.axis_index("pair")
    shard_width = occ_coef.shape[1]
    occ_total = shard_width * lax.axis_size("occ")
    slot_occupied_flag, slot_lambda_block, slot_sigma_block = slot_lookup_table(
        screened_block_mask, tile_holder_pair, pair_count * tile_slots, tile_slots
    )
    occ_used = trim_rows(occ_coef, shell_size, slot_width)
    vir_used = trim_rows(vir_coef, shell_size, slot_width)
    block_ids = jnp.arange(block_count, dtype=jnp.int32)
    placing = (
        (slot_sigma_block[:, None] == block_ids[None, :]) & (slot_occupied_flag[:, None] > 0)
    ).astype(jnp.bfloat16)
    own_lam = lax.dynamic_slice_in_dim(slot_lambda_block, pair_index * tile_slots, tile_slots)
    panel_whole = lax.all_gather(occ_used, "occ", axis=1, tiled=True)
    panel_rows = panel_whole.reshape(block_count, slot_width, occ_total)[own_lam]
    tile_parts = jnp.einsum(
        "rkls,klj->krjs", quarter_integrals, panel_rows, preferred_element_type=jnp.float32
    ).astype(jnp.bfloat16)
    summed = spread_tiles(
        placing, lax.all_to_all(tile_parts, "pair", split_axis=2, concat_axis=0, tiled=True)
    )
    half_mo = summed.astype(jnp.bfloat16)
    return jnp.einsum(
        "rjs,sb->rjb",
        lax.all_gather(half_mo, "occ", axis=0, tiled=True),
        vir_used,
        preferred_element_type=jnp.float32,
    ).astype(jnp.bfloat16)


def transform_kernel(
    lam_ref, rank_ref, used_ref, pairs_ref, integrals_ref, panel_ref, vir_ref, out_ref, half_ref
):
    n_pair, _, tile_slots, width, _ = integrals_ref.shape[1:]
    half_ref[...] = jnp.zeros_like(half_ref)
    for p in range(n_pair):
        for k in range(tile_slots):
            t = p * tile_slots + k

            @pl.when(used_ref[t] > 0)
            def _():
                lam = pl.multiple_of(lam_ref[t] * width, width)
                place = pl.ds(pl.multiple_of(rank_ref[t] * width, width), width)
                half_ref[:, place] += jnp.dot(
                    panel_ref[:, pl.ds(lam, width)],
                    integrals_ref[0, p, 0, k],
                    preferred_element_type=jnp.float32,
                )

    total = half_ref.shape[1]
    step = min(2 * width, total)
    for n in range(1, -(-total // step) + 1):
        depth = min(n * step, total)

        @pl.when(pairs_ref[0] == n)
        def _():
            out_ref[0] = jnp.dot(
                half_ref[:, :depth].astype(jnp.bfloat16),
                vir_ref[:depth, :],
                preferred_element_type=jnp.float32,
            ).astype(out_ref.dtype)


def transform(lam, rank, used, pairs, integrals, panel, vir):
    n_occ, n_pair, rows, tile_slots, width, _ = integrals.shape
    columns, total = panel.shape
    virtuals = vir.shape[1]
    return pl.pallas_call(
        transform_kernel,
        out_shape=jax.ShapeDtypeStruct((n_occ * rows, columns, virtuals), jnp.bfloat16),
        grid_spec=pltpu.PrefetchScalarGridSpec(
            num_scalar_prefetch=4,
            grid=(n_occ * rows,),
            in_specs=[
                pl.BlockSpec(
                    (1, n_pair, 1, tile_slots, width, width),
                    lambda r, *_: (r // rows, 0, r % rows, 0, 0, 0),
                ),
                pl.BlockSpec((columns, total), lambda r, *_: (0, 0)),
                pl.BlockSpec((total, virtuals), lambda r, *_: (0, 0)),
            ],
            out_specs=pl.BlockSpec((1, columns, virtuals), lambda r, *_: (r, 0, 0)),
            scratch_shapes=[pltpu.VMEM((columns, total), jnp.float32)],
        ),
        compiler_params=pltpu.CompilerParams(vmem_limit_bytes=48 * 2**20),
    )(lam, rank, used, pairs, integrals, panel, vir)


def own_panel(occ_coef, mesh_shape):
    n_pair, n_occ = mesh_shape["pair"], mesh_shape["occ"]
    parts = n_pair // n_occ
    width = occ_coef.shape[1] // parts
    part = lax.rem(lax.axis_index("pair"), parts)
    sent = lax.dynamic_slice_in_dim(occ_coef, part * width, width, axis=1)
    moves = [
        (a * n_occ + b, (b * parts + a % parts) * n_occ + a // parts)
        for a in range(n_pair)
        for b in range(n_occ)
    ]
    return lax.ppermute(sent, ("pair", "occ"), moves)


def send_integrals(
    mesh_shape,
    quarter_integrals,
    occ_coef,
    vir_coef,
    screened_block_mask,
    tile_holder_pair,
    shell_size,
):
    n_pair, n_occ = mesh_shape["pair"], mesh_shape["occ"]
    block_count = screened_block_mask.shape[0]
    rows, tile_slots, slot_width, _ = quarter_integrals.shape
    gathered = lax.all_gather(quarter_integrals, ("occ", "pair"), axis=0, tiled=False)
    gathered = gathered.reshape((n_occ, n_pair) + quarter_integrals.shape)
    panel = trim_rows(own_panel(occ_coef, mesh_shape), shell_size, slot_width).T
    used, lam, sig = slot_lookup_table(
        screened_block_mask, tile_holder_pair, n_pair * tile_slots, tile_slots
    )
    blocks = jnp.arange(block_count, dtype=jnp.int32)
    present = jnp.any((sig[:, None] == blocks[None, :]) & (used[:, None] > 0), axis=0)
    before = present[None, :] & (blocks[None, :] < blocks[:, None])
    rank_of = jnp.sum(before.astype(jnp.int32), axis=1)
    rank = jnp.sum((sig[:, None] == blocks[None, :]) * rank_of[None, :], axis=1)
    held = (rank_of[None, :] == blocks[:, None]) & present[None, :]
    block_at = jnp.sum(held * blocks[None, :], axis=1)
    pairs = (jnp.sum(present.astype(jnp.int32)) + 1) // 2
    inside = jnp.arange(slot_width, dtype=jnp.int32)[None, :] < shell_size[block_at][:, None]
    vir = vir_coef.reshape(block_count, slot_width, -1)[block_at]
    vir = jnp.where(inside[:, :, None], vir, jnp.zeros((), vir.dtype)).reshape(vir_coef.shape)
    return transform(lam, rank, used, pairs.reshape(1), gathered, panel, vir)


def pick_plan(mesh_shape):
    n_pair, n_occ = mesh_shape["pair"], mesh_shape["occ"]

    def per_device(quarter_integrals, occ_coef, vir_coef, *tables):
        rows, tile_slots, width, _ = quarter_integrals.shape
        columns = occ_coef.shape[1] * n_occ // n_pair
        integrals = n_occ * n_pair * quarter_integrals.size
        transformed = rows * columns * (
            n_pair * tile_slots * width + n_occ * occ_coef.shape[0]
        )
        if n_pair % n_occ == 0 and integrals < transformed:
            plan = functools.partial(send_integrals, mesh_shape)
        else:
            plan = send_tiles
        return plan(quarter_integrals, occ_coef, vir_coef, *tables)

    return per_device


def solution(mesh):
    placed = (
        P(("frag", "occ"), "pair", None, None),
        P("frag", "occ"),
        P("frag", "occ"),
        P("frag", None),
        P("frag", None),
        P("frag"),
    )
    return jax.shard_map(
        pick_plan(dict(mesh.shape)), mesh=mesh, in_specs=placed, out_specs=P("frag", "pair", "occ"), check_vma=False
    )
```

```python
import functools

import jax
import jax.numpy as jnp
from jax import lax
from jax.experimental import pallas as pl
from jax.experimental.pallas import tpu as pltpu
from jax.sharding import PartitionSpec as P


def slot_lookup_table(screened_block_mask, tile_holder_pair, slot_count, tile_slots):
    block_count = screened_block_mask.shape[0]
    kept_tiles = screened_block_mask.reshape(-1)
    owners = tile_holder_pair.reshape(-1)
    tile_index = jnp.arange(kept_tiles.shape[0], dtype=jnp.int32)
    earlier = (
        (owners[:, None] == owners[None, :])
        & (tile_index[None, :] < tile_index[:, None])
        & (kept_tiles[None, :] == 1)
    )
    rank_within = jnp.sum(earlier.astype(jnp.int32), axis=1)
    slot_of = owners * tile_slots + rank_within
    slot_index = jnp.arange(slot_count, dtype=jnp.int32)
    holding = ((slot_of[None, :] == slot_index[:, None]) & (kept_tiles[None, :] == 1)).astype(
        jnp.int32
    )
    slot_occupied_flag = jnp.sum(holding, axis=1)
    slot_lambda_block = jnp.sum(holding * (tile_index // block_count)[None, :], axis=1)
    slot_sigma_block = jnp.sum(holding * (tile_index % block_count)[None, :], axis=1)
    return (slot_occupied_flag, slot_lambda_block, slot_sigma_block)


def trim_rows(coefficients, shell_size, slot_width):
    inside = jnp.arange(slot_width, dtype=jnp.int32)[None, :] < shell_size[:, None]
    return jnp.where(inside.reshape(-1)[:, None], coefficients, jnp.zeros((), coefficients.dtype))


def spread_tiles(placing, tile_parts):
    spread = jnp.einsum("kn,krjs->rjns", placing, tile_parts, preferred_element_type=jnp.float32)
    return spread.reshape(spread.shape[0], spread.shape[1], -1)


def send_tiles(
    quarter_integrals, occ_coef, vir_coef, screened_block_mask, tile_holder_pair, shell_size
):
    block_count = screened_block_mask.shape[0]
    slot_width = quarter_integrals.shape[3]
    tile_slots = quarter_integrals.shape[1]
    pair_count = lax.axis_size("pair")
    pair_index = lax.axis_index("pair")
    shard_width = occ_coef.shape[1]
    occ_total = shard_width * lax.axis_size("occ")
    slot_occupied_flag, slot_lambda_block, slot_sigma_block = slot_lookup_table(
        screened_block_mask, tile_holder_pair, pair_count * tile_slots, tile_slots
    )
    occ_used = trim_rows(occ_coef, shell_size, slot_width)
    vir_used = trim_rows(vir_coef, shell_size, slot_width)
    block_ids = jnp.arange(block_count, dtype=jnp.int32)
    placing = (
        (slot_sigma_block[:, None] == block_ids[None, :]) & (slot_occupied_flag[:, None] > 0)
    ).astype(jnp.bfloat16)
    own_lam = lax.dynamic_slice_in_dim(slot_lambda_block, pair_index * tile_slots, tile_slots)
    panel_whole = lax.all_gather(occ_used, "occ", axis=1, tiled=True)
    panel_rows = panel_whole.reshape(block_count, slot_width, occ_total)[own_lam]
    tile_parts = jnp.einsum(
        "rkls,klj->krjs", quarter_integrals, panel_rows, preferred_element_type=jnp.float32
    ).astype(jnp.bfloat16)
    summed = spread_tiles(
        placing, lax.all_to_all(tile_parts, "pair", split_axis=2, concat_axis=0, tiled=True)
    )
    half_mo = summed.astype(jnp.bfloat16)
    return jnp.einsum(
        "rjs,sb->rjb",
        lax.all_gather(half_mo, "occ", axis=0, tiled=True),
        vir_used,
        preferred_element_type=jnp.float32,
    ).astype(jnp.bfloat16)


MESH = pl.DeviceIdType.MESH


def gather_kernel(
    n_pair, n_occ, integrals_ref, shard_ref, all_ref, panel_ref, local, z_send, z_recv,
    x_send, x_recv, core_send, core_recv, panel_send, panel_recv,
):
    cores = 2
    n_x = n_occ // cores
    z, occ = lax.axis_index("pair"), lax.axis_index("occ")
    x, core = occ // cores, lax.rem(occ, cores)
    sibling = x * cores + 1 - core
    holder = z // (n_pair // n_occ)
    holder_x, holder_core = holder // cores, lax.rem(holder, cores)
    z_peers = [lax.rem(z + d, n_pair) for d in range(1, n_pair)]
    x_peers = [lax.rem(x + d, n_x) for d in range(1, n_x)]

    barrier = pltpu.get_barrier_semaphore()
    for peer in z_peers:
        pl.semaphore_signal(barrier, inc=1, device_id={"pair": peer}, device_id_type=MESH)
    for peer in x_peers:
        pl.semaphore_signal(
            barrier, inc=1, device_id={"occ": peer * cores + core}, device_id_type=MESH
        )
    pl.semaphore_signal(barrier, inc=1, device_id={"occ": sibling}, device_id_type=MESH)
    pl.semaphore_wait(barrier, n_pair + n_x - 1)

    def along_z(d):
        return pltpu.make_async_remote_copy(
            src_ref=integrals_ref,
            dst_ref=all_ref.at[occ, z],
            send_sem=z_send.at[d],
            recv_sem=z_recv.at[d],
            device_id={"pair": lax.rem(z + d, n_pair)},
            device_id_type=MESH,
        )

    def block(x_of, d):
        return all_ref.at[x_of * cores + core, lax.rem(z + n_pair - d, n_pair)]

    def across_x(e, d):
        source = integrals_ref if d == 0 else block(x, d)
        return pltpu.make_async_remote_copy(
            src_ref=source,
            dst_ref=block(x, d),
            send_sem=x_send.at[e, d],
            recv_sem=x_recv.at[e, d],
            device_id={"occ": lax.rem(x + e, n_x) * cores + core},
            device_id_type=MESH,
        )

    def across_cores(e, d):
        x_of = lax.rem(x + n_x - e, n_x)
        source = integrals_ref if d == 0 and e == 0 else block(x_of, d)
        return pltpu.make_async_remote_copy(
            src_ref=source,
            dst_ref=block(x_of, d),
            send_sem=core_send.at[e, d],
            recv_sem=core_recv.at[e, d],
            device_id={"occ": sibling},
            device_id_type=MESH,
        )

    def panel_to(place, source, target):
        return pltpu.make_async_remote_copy(
            src_ref=source,
            dst_ref=panel_ref,
            send_sem=panel_send.at[place],
            recv_sem=panel_recv,
            device_id={"occ": target},
            device_id_type=MESH,
        )

    holds = occ == holder
    passes_on = jnp.logical_and(core == holder_core, x != holder_x)

    for d in range(1, n_pair):
        along_z(d).start()
    for e in range(1, n_x):
        across_x(e, 0).start()
    own = pltpu.make_async_copy(integrals_ref, all_ref.at[occ, z], local.at[0])
    own.start()
    own_panel = pltpu.make_async_copy(shard_ref, panel_ref, local.at[1])

    @pl.when(holds)
    def _():
        for e in range(1, n_x):
            panel_to(e, shard_ref, lax.rem(x + e, n_x) * cores + core).start()
        panel_to(0, shard_ref, sibling).start()
        own_panel.start()

    across_cores(0, 0).start()
    for d in range(1, n_pair):
        along_z(d).wait_recv()
        for e in range(1, n_x):
            across_x(e, d).start()
        across_cores(0, d).start()

    @pl.when(passes_on)
    def _():
        panel_to(0, panel_ref, sibling).wait_recv()
        panel_to(0, panel_ref, sibling).start()

    for d in range(n_pair):
        for e in range(1, n_x):
            across_x(e, d).wait_recv()
            across_cores(e, d).start()

    @pl.when(core != holder_core)
    def _():
        panel_to(0, panel_ref, sibling).wait_recv()

    for e in range(n_x):
        for d in range(n_pair):
            across_cores(e, d).wait()
    for e in range(1, n_x):
        for d in range(n_pair):
            across_x(e, d).wait_send()
    for d in range(1, n_pair):
        along_z(d).wait_send()
    own.wait()

    @pl.when(holds)
    def _():
        for e in range(1, n_x):
            panel_to(e, shard_ref, sibling).wait_send()
        panel_to(0, shard_ref, sibling).wait_send()
        own_panel.wait()

    @pl.when(passes_on)
    def _():
        panel_to(0, panel_ref, sibling).wait_send()


def gather(mesh_shape, integrals, shard):
    n_pair, n_occ = mesh_shape["pair"], mesh_shape["occ"]
    n_x = n_occ // 2
    return pl.pallas_call(
        functools.partial(gather_kernel, n_pair, n_occ),
        out_shape=(
            jax.ShapeDtypeStruct((n_occ, n_pair) + integrals.shape, integrals.dtype),
            jax.ShapeDtypeStruct(shard.shape, shard.dtype),
        ),
        in_specs=[pl.BlockSpec(memory_space=pl.ANY)] * 2,
        out_specs=(pl.BlockSpec(memory_space=pl.ANY),) * 2,
        scratch_shapes=[
            pltpu.SemaphoreType.DMA((2,)),
            pltpu.SemaphoreType.DMA((n_pair,)),
            pltpu.SemaphoreType.DMA((n_pair,)),
            pltpu.SemaphoreType.DMA((n_x, n_pair)),
            pltpu.SemaphoreType.DMA((n_x, n_pair)),
            pltpu.SemaphoreType.DMA((n_x, n_pair)),
            pltpu.SemaphoreType.DMA((n_x, n_pair)),
            pltpu.SemaphoreType.DMA((n_x,)),
            pltpu.SemaphoreType.DMA,
        ],
        compiler_params=pltpu.CompilerParams(collective_id=0, has_side_effects=True),
    )(integrals, shard)


def transform_kernel(
    lam_ref, rank_ref, used_ref, at_ref, size_ref, count_ref,
    integrals_ref, panel_ref, vir_ref, out_ref, half_ref, kept_ref,
):
    n_pair, rows, tile_slots, width, _ = integrals_ref.shape[1:]
    columns, total = panel_ref.shape
    step = min(2 * width, total)

    @pl.when(pl.program_id(0) == 0)
    def _():
        kept_ref[...] = jnp.zeros_like(kept_ref)
        for i in range(total // width):

            @pl.when(i < count_ref[0])
            def _():
                block = at_ref[i]
                shape = (width, vir_ref.shape[1])
                inside = lax.broadcasted_iota(jnp.int32, shape, 0) < size_ref[block]
                found = vir_ref[pl.ds(pl.multiple_of(block * width, width), width), :]
                kept_ref[i * width : (i + 1) * width, :] = jnp.where(
                    inside, found.astype(jnp.float32), 0.0
                ).astype(kept_ref.dtype)

    half_ref[...] = jnp.zeros_like(half_ref)
    for p in range(n_pair):
        for k in range(tile_slots):
            t = p * tile_slots + k

            @pl.when(used_ref[t] > 0)
            def _():
                lam = pl.multiple_of(lam_ref[t] * width, width)
                place = pl.ds(pl.multiple_of(rank_ref[t] * width, width), width)
                tiles = jnp.concatenate([integrals_ref[0, p, r, k] for r in range(rows)], axis=1)
                part = jnp.dot(
                    panel_ref[:, pl.ds(lam, width)], tiles, preferred_element_type=jnp.float32
                )
                for r in range(rows):
                    half_ref[r, :, place] += part[:, r * width : (r + 1) * width]

    for n in range(1, -(-total // step) + 1):
        depth = min(n * step, total)

        @pl.when((count_ref[0] * width + step - 1) // step == n)
        def _():
            for r in range(rows):
                out_ref[r] = jnp.dot(
                    half_ref[r, :, :depth].astype(jnp.bfloat16),
                    kept_ref[:depth, :],
                    preferred_element_type=jnp.float32,
                ).astype(out_ref.dtype)


def transform(lam, rank, used, block_at, shell_size, count, integrals, panel, vir):
    n_occ, n_pair, rows, tile_slots, width, _ = integrals.shape
    columns, total = panel.shape
    virtuals = vir.shape[1]
    return pl.pallas_call(
        transform_kernel,
        out_shape=jax.ShapeDtypeStruct((n_occ * rows, columns, virtuals), jnp.bfloat16),
        grid_spec=pltpu.PrefetchScalarGridSpec(
            num_scalar_prefetch=6,
            grid=(n_occ,),
            in_specs=[
                pl.BlockSpec(
                    (1, n_pair, rows, tile_slots, width, width),
                    lambda o, *_: (o, 0, 0, 0, 0, 0),
                ),
                pl.BlockSpec((columns, total), lambda o, *_: (0, 0)),
                pl.BlockSpec((total, virtuals), lambda o, *_: (0, 0)),
            ],
            out_specs=pl.BlockSpec((rows, columns, virtuals), lambda o, *_: (o, 0, 0)),
            scratch_shapes=[
                pltpu.VMEM((rows, columns, total), jnp.float32),
                pltpu.VMEM((total, virtuals), jnp.bfloat16),
            ],
        ),
        compiler_params=pltpu.CompilerParams(vmem_limit_bytes=56 * 2**20),
    )(lam, rank, used, block_at, shell_size, count, integrals, panel, vir)


def send_integrals(
    mesh_shape,
    quarter_integrals,
    occ_coef,
    vir_coef,
    screened_block_mask,
    tile_holder_pair,
    shell_size,
):
    n_pair, n_occ = mesh_shape["pair"], mesh_shape["occ"]
    block_count = screened_block_mask.shape[0]
    rows, tile_slots, slot_width, _ = quarter_integrals.shape
    parts = n_pair // n_occ
    shard = occ_coef
    if parts > 1:
        wide = occ_coef.shape[1] // parts
        part = lax.rem(lax.axis_index("pair"), parts)
        shard = lax.dynamic_slice_in_dim(occ_coef, part * wide, wide, axis=1)
    gathered, panel = gather(mesh_shape, quarter_integrals, shard)
    panel = trim_rows(panel, shell_size, slot_width).T
    used, lam, sig = slot_lookup_table(
        screened_block_mask, tile_holder_pair, n_pair * tile_slots, tile_slots
    )
    blocks = jnp.arange(block_count, dtype=jnp.int32)
    present = jnp.any((sig[:, None] == blocks[None, :]) & (used[:, None] > 0), axis=0)
    before = present[None, :] & (blocks[None, :] < blocks[:, None])
    rank_of = jnp.sum(before.astype(jnp.int32), axis=1)
    rank = jnp.sum((sig[:, None] == blocks[None, :]) * rank_of[None, :], axis=1)
    held = (rank_of[None, :] == blocks[:, None]) & present[None, :]
    block_at = jnp.sum(held * blocks[None, :], axis=1)
    count = jnp.sum(present.astype(jnp.int32)).reshape(1)
    return transform(
        lam, rank, used, block_at, shell_size, count, gathered, panel, vir_coef
    )


def pick_plan(mesh_shape):
    n_pair, n_occ = mesh_shape["pair"], mesh_shape["occ"]

    def per_device(quarter_integrals, occ_coef, vir_coef, *tables):
        rows, tile_slots, width, _ = quarter_integrals.shape
        columns = occ_coef.shape[1] * n_occ // n_pair
        integrals = n_occ * n_pair * quarter_integrals.size
        transformed = rows * columns * (
            n_pair * tile_slots * width + n_occ * occ_coef.shape[0]
        )
        if n_occ % 2 == 0 and n_pair % n_occ == 0 and integrals < transformed:
            plan = functools.partial(send_integrals, mesh_shape)
        else:
            plan = send_tiles
        return plan(quarter_integrals, occ_coef, vir_coef, *tables)

    return per_device


def solution(mesh):
    placed = (
        P(("frag", "occ"), "pair", None, None),
        P("frag", "occ"),
        P("frag", "occ"),
        P("frag", None),
        P("frag", None),
        P("frag"),
    )
    return jax.shard_map(
        pick_plan(dict(mesh.shape)), mesh=mesh, in_specs=placed, out_specs=P("frag", "pair", "occ"), check_vma=False
    )
```

```python
import functools

import jax
import jax.numpy as jnp
from jax import lax
from jax.experimental import pallas as pl
from jax.experimental.pallas import tpu as pltpu
from jax.sharding import PartitionSpec as P


def slot_lookup_table(screened_block_mask, tile_holder_pair, slot_count, tile_slots):
    block_count = screened_block_mask.shape[0]
    kept_tiles = screened_block_mask.reshape(-1)
    owners = tile_holder_pair.reshape(-1)
    tile_index = jnp.arange(kept_tiles.shape[0], dtype=jnp.int32)
    earlier = (
        (owners[:, None] == owners[None, :])
        & (tile_index[None, :] < tile_index[:, None])
        & (kept_tiles[None, :] == 1)
    )
    rank_within = jnp.sum(earlier.astype(jnp.int32), axis=1)
    slot_of = owners * tile_slots + rank_within
    slot_index = jnp.arange(slot_count, dtype=jnp.int32)
    holding = ((slot_of[None, :] == slot_index[:, None]) & (kept_tiles[None, :] == 1)).astype(
        jnp.int32
    )
    slot_occupied_flag = jnp.sum(holding, axis=1)
    slot_lambda_block = jnp.sum(holding * (tile_index // block_count)[None, :], axis=1)
    slot_sigma_block = jnp.sum(holding * (tile_index % block_count)[None, :], axis=1)
    return (slot_occupied_flag, slot_lambda_block, slot_sigma_block)


def trim_rows(coefficients, shell_size, slot_width):
    inside = jnp.arange(slot_width, dtype=jnp.int32)[None, :] < shell_size[:, None]
    return jnp.where(inside.reshape(-1)[:, None], coefficients, jnp.zeros((), coefficients.dtype))


def spread_tiles(placing, tile_parts):
    spread = jnp.einsum("kn,krjs->rjns", placing, tile_parts, preferred_element_type=jnp.float32)
    return spread.reshape(spread.shape[0], spread.shape[1], -1)


def send_tiles(
    quarter_integrals, occ_coef, vir_coef, screened_block_mask, tile_holder_pair, shell_size
):
    block_count = screened_block_mask.shape[0]
    slot_width = quarter_integrals.shape[3]
    tile_slots = quarter_integrals.shape[1]
    pair_count = lax.axis_size("pair")
    pair_index = lax.axis_index("pair")
    shard_width = occ_coef.shape[1]
    occ_total = shard_width * lax.axis_size("occ")
    slot_occupied_flag, slot_lambda_block, slot_sigma_block = slot_lookup_table(
        screened_block_mask, tile_holder_pair, pair_count * tile_slots, tile_slots
    )
    occ_used = trim_rows(occ_coef, shell_size, slot_width)
    vir_used = trim_rows(vir_coef, shell_size, slot_width)
    block_ids = jnp.arange(block_count, dtype=jnp.int32)
    placing = (
        (slot_sigma_block[:, None] == block_ids[None, :]) & (slot_occupied_flag[:, None] > 0)
    ).astype(jnp.bfloat16)
    own_lam = lax.dynamic_slice_in_dim(slot_lambda_block, pair_index * tile_slots, tile_slots)
    panel_whole = lax.all_gather(occ_used, "occ", axis=1, tiled=True)
    panel_rows = panel_whole.reshape(block_count, slot_width, occ_total)[own_lam]
    tile_parts = jnp.einsum(
        "rkls,klj->krjs", quarter_integrals, panel_rows, preferred_element_type=jnp.float32
    ).astype(jnp.bfloat16)
    summed = spread_tiles(
        placing, lax.all_to_all(tile_parts, "pair", split_axis=2, concat_axis=0, tiled=True)
    )
    half_mo = summed.astype(jnp.bfloat16)
    return jnp.einsum(
        "rjs,sb->rjb",
        lax.all_gather(half_mo, "occ", axis=0, tiled=True),
        vir_used,
        preferred_element_type=jnp.float32,
    ).astype(jnp.bfloat16)


MESH = pl.DeviceIdType.MESH


def gather_kernel(
    n_pair, n_occ, size_ref, mask_ref, owner_ref, integrals_ref, shard_ref,
    all_ref, turned_ref, slots_ref, panel_ref, local, z_send, z_recv, x_send, x_recv,
    core_send, core_recv, panel_send, panel_recv,
):
    cores = 2
    n_x = n_occ // cores
    z, occ = lax.axis_index("pair"), lax.axis_index("occ")
    x, core = occ // cores, lax.rem(occ, cores)
    sibling = x * cores + 1 - core
    holder = z // (n_pair // n_occ)
    holder_x, holder_core = holder // cores, lax.rem(holder, cores)
    z_peers = [lax.rem(z + d, n_pair) for d in range(1, n_pair)]
    x_peers = [lax.rem(x + d, n_x) for d in range(1, n_x)]

    barrier = pltpu.get_barrier_semaphore()
    for peer in z_peers:
        pl.semaphore_signal(barrier, inc=1, device_id={"pair": peer}, device_id_type=MESH)
    for peer in x_peers:
        pl.semaphore_signal(
            barrier, inc=1, device_id={"occ": peer * cores + core}, device_id_type=MESH
        )
    pl.semaphore_signal(barrier, inc=1, device_id={"occ": sibling}, device_id_type=MESH)
    pl.semaphore_wait(barrier, n_pair + n_x - 1)

    def along_z(d):
        return pltpu.make_async_remote_copy(
            src_ref=integrals_ref,
            dst_ref=all_ref.at[occ, z],
            send_sem=z_send.at[d],
            recv_sem=z_recv.at[d],
            device_id={"pair": lax.rem(z + d, n_pair)},
            device_id_type=MESH,
        )

    def block(x_of, d):
        return all_ref.at[x_of * cores + core, lax.rem(z + n_pair - d, n_pair)]

    def across_x(e, d):
        source = integrals_ref if d == 0 else block(x, d)
        return pltpu.make_async_remote_copy(
            src_ref=source,
            dst_ref=block(x, d),
            send_sem=x_send.at[e, d],
            recv_sem=x_recv.at[e, d],
            device_id={"occ": lax.rem(x + e, n_x) * cores + core},
            device_id_type=MESH,
        )

    def across_cores(e, d):
        x_of = lax.rem(x + n_x - e, n_x)
        source = integrals_ref if d == 0 and e == 0 else block(x_of, d)
        return pltpu.make_async_remote_copy(
            src_ref=source,
            dst_ref=block(x_of, d),
            send_sem=core_send.at[e, d],
            recv_sem=core_recv.at[e, d],
            device_id={"occ": sibling},
            device_id_type=MESH,
        )

    def panel_to(place, source, target):
        return pltpu.make_async_remote_copy(
            src_ref=source,
            dst_ref=panel_ref,
            send_sem=panel_send.at[place],
            recv_sem=panel_recv,
            device_id={"occ": target},
            device_id_type=MESH,
        )

    holds = occ == holder
    passes_on = jnp.logical_and(core == holder_core, x != holder_x)

    for d in range(1, n_pair):
        along_z(d).start()
    own = pltpu.make_async_copy(integrals_ref, all_ref.at[occ, z], local.at[0])
    own.start()
    own_panel = pltpu.make_async_copy(shard_ref, panel_ref, local.at[1])

    @pl.when(holds)
    def _():
        for e in range(1, n_x):
            panel_to(e, shard_ref, lax.rem(x + e, n_x) * cores + core).start()
        panel_to(0, shard_ref, sibling).start()
        own_panel.start()

    for e in range(1, n_x):
        across_x(e, 0).start()
    across_cores(0, 0).start()
    write_slots(n_pair, mask_ref, owner_ref, slots_ref)
    for d in range(1, n_pair):
        along_z(d).wait_recv()
        for e in range(1, n_x):
            across_x(e, d).start()
        across_cores(0, d).start()

    @pl.when(passes_on)
    def _():
        panel_to(0, panel_ref, sibling).wait_recv()
        panel_to(0, panel_ref, sibling).start()

    @pl.when(core != holder_core)
    def _():
        panel_to(0, panel_ref, sibling).wait_recv()

    @pl.when(holds)
    def _():
        own_panel.wait()

    turn_panel(size_ref, panel_ref, turned_ref)
    for d in range(n_pair):
        for e in range(1, n_x):
            across_x(e, d).wait_recv()
            across_cores(e, d).start()

    for e in range(n_x):
        for d in range(n_pair):
            across_cores(e, d).wait()
    for e in range(1, n_x):
        for d in range(n_pair):
            across_x(e, d).wait_send()
    for d in range(1, n_pair):
        along_z(d).wait_send()
    own.wait()

    @pl.when(holds)
    def _():
        for e in range(1, n_x):
            panel_to(e, shard_ref, sibling).wait_send()
        panel_to(0, shard_ref, sibling).wait_send()

    @pl.when(passes_on)
    def _():
        panel_to(0, panel_ref, sibling).wait_send()


def gather(mesh_shape, shell_size, mask, owner, integrals, shard):
    n_pair, n_occ = mesh_shape["pair"], mesh_shape["occ"]
    n_x = n_occ // 2
    slots = n_pair * integrals.shape[1]
    return pl.pallas_call(
        functools.partial(gather_kernel, n_pair, n_occ),
        out_shape=(
            jax.ShapeDtypeStruct((n_occ, n_pair) + integrals.shape, integrals.dtype),
            jax.ShapeDtypeStruct(shard.shape[::-1], shard.dtype),
            jax.ShapeDtypeStruct((3 * slots,), jnp.int32),
        ),
        in_specs=[
            pl.BlockSpec(memory_space=pltpu.SMEM),
            pl.BlockSpec(memory_space=pltpu.VMEM),
            pl.BlockSpec(memory_space=pltpu.VMEM),
            pl.BlockSpec(memory_space=pl.ANY),
            pl.BlockSpec(memory_space=pl.ANY),
        ],
        out_specs=(
            pl.BlockSpec(memory_space=pl.ANY),
            pl.BlockSpec(memory_space=pltpu.VMEM),
            pl.BlockSpec(memory_space=pltpu.SMEM),
        ),
        scratch_shapes=[
            pltpu.VMEM(shard.shape, shard.dtype),
            pltpu.SemaphoreType.DMA((2,)),
            pltpu.SemaphoreType.DMA((n_pair,)),
            pltpu.SemaphoreType.DMA((n_pair,)),
            pltpu.SemaphoreType.DMA((n_x, n_pair)),
            pltpu.SemaphoreType.DMA((n_x, n_pair)),
            pltpu.SemaphoreType.DMA((n_x, n_pair)),
            pltpu.SemaphoreType.DMA((n_x, n_pair)),
            pltpu.SemaphoreType.DMA((n_x,)),
            pltpu.SemaphoreType.DMA,
        ],
        compiler_params=pltpu.CompilerParams(
            collective_id=0, has_side_effects=True, vmem_limit_bytes=24 * 2**20
        ),
    )(shell_size, mask, owner, integrals, shard)


def write_slots(n_pair, mask_ref, owner_ref, slots_ref):
    shape = mask_ref.shape
    tile_slots = slots_ref.shape[0] // (3 * n_pair)
    row = lax.broadcasted_iota(jnp.int32, shape, 0)
    column = lax.broadcasted_iota(jnp.int32, shape, 1)
    before = (row < column).astype(jnp.float32)
    kept, owner = mask_ref[...] == 1, owner_ref[...]
    rows_of, columns_of = row.astype(jnp.float32), column.astype(jnp.float32)
    for p in range(n_pair):
        owned = (kept & (owner == p)).astype(jnp.float32)
        in_row = jnp.dot(owned, before, preferred_element_type=jnp.float32)
        sums = jnp.broadcast_to(jnp.sum(owned, axis=1, keepdims=True), shape)
        above = jnp.zeros(shape, jnp.float32)
        for i in range(shape[0]):
            above += jnp.where(row > i, sums[i : i + 1, :], 0.0)
        rank = in_row + above
        for k in range(tile_slots):
            chosen = jnp.where(rank == float(k), owned, 0.0)
            t = p * tile_slots + k
            slots_ref[3 * t] = jnp.sum(chosen).astype(jnp.int32)
            slots_ref[3 * t + 1] = jnp.sum(chosen * rows_of).astype(jnp.int32)
            slots_ref[3 * t + 2] = jnp.sum(chosen * columns_of).astype(jnp.int32)


def turn_panel(size_ref, panel_ref, turned_ref):
    total, columns = panel_ref.shape
    blocks = size_ref.shape[0]
    width = total // blocks
    place = lax.broadcasted_iota(jnp.int32, (width, columns), 0)
    for i in range(blocks):
        found = panel_ref[i * width : (i + 1) * width, :].astype(jnp.float32)
        used = jnp.where(place < size_ref[i], found, 0.0)
        turned_ref[:, i * width : (i + 1) * width] = used.T.astype(turned_ref.dtype)


def transform_kernel(
    slots_ref, size_ref, integrals_ref, panel_ref, vir_ref, out_ref,
    half_ref, kept_ref, rank_ref, first_ref, at_ref, count_ref,
):
    n_pair, rows, tile_slots, width, _ = integrals_ref.shape[1:]
    columns, total = panel_ref.shape
    blocks = total // width
    step = min(2 * width, total)

    @pl.when(pl.program_id(0) == 0)
    def _():
        count = jnp.int32(0)
        for t in range(n_pair * tile_slots):
            sig, rank, first = slots_ref[3 * t + 2], count, jnp.int32(1)
            for u in range(t):
                same = (slots_ref[3 * u] > 0) & (slots_ref[3 * u + 2] == sig)
                rank = jnp.where(same, rank_ref[u], rank)
                first = jnp.where(same, 0, first)
            rank_ref[t] = rank
            first_ref[t] = first
            at_ref[count] = sig
            count += first * slots_ref[3 * t]
        count_ref[0] = count
        half_ref[...] = jnp.zeros_like(half_ref)
        for i in range(blocks):

            @pl.when(i < count)
            def _():
                block = at_ref[i]
                shape = (width, vir_ref.shape[1])
                inside = lax.broadcasted_iota(jnp.int32, shape, 0) < size_ref[block]
                found = vir_ref[pl.ds(pl.multiple_of(block * width, width), width), :]
                kept_ref[i * width : (i + 1) * width, :] = jnp.where(
                    inside, found.astype(jnp.float32), 0.0
                ).astype(kept_ref.dtype)

            @pl.when(i >= count)
            def _():
                kept_ref[i * width : (i + 1) * width, :] = jnp.zeros(
                    (width, vir_ref.shape[1]), kept_ref.dtype
                )

    for p in range(n_pair):
        for k in range(tile_slots):
            t = p * tile_slots + k

            @pl.when(slots_ref[3 * t] > 0)
            def _():
                lam = pl.multiple_of(slots_ref[3 * t + 1] * width, width)
                place = pl.ds(pl.multiple_of(rank_ref[t] * width, width), width)
                tiles = jnp.concatenate([integrals_ref[0, p, r, k] for r in range(rows)], axis=1)
                part = jnp.dot(
                    panel_ref[:, pl.ds(lam, width)], tiles, preferred_element_type=jnp.float32
                )

                @pl.when(first_ref[t] > 0)
                def _():
                    for r in range(rows):
                        half_ref[r * columns : (r + 1) * columns, place] = part[
                            :, r * width : (r + 1) * width
                        ]

                @pl.when(first_ref[t] == 0)
                def _():
                    for r in range(rows):
                        half_ref[r * columns : (r + 1) * columns, place] += part[
                            :, r * width : (r + 1) * width
                        ]

    for n in range(1, -(-total // step) + 1):
        depth = min(n * step, total)

        @pl.when((count_ref[0] * width + step - 1) // step == n)
        def _():
            out_ref[...] = (
                jnp.dot(
                    half_ref[:, :depth].astype(jnp.bfloat16),
                    kept_ref[:depth, :],
                    preferred_element_type=jnp.float32,
                )
                .astype(out_ref.dtype)
                .reshape(out_ref.shape)
            )


def transform(slots, shell_size, integrals, panel, vir):
    n_occ, n_pair, rows, tile_slots, width, _ = integrals.shape
    columns, total = panel.shape
    virtuals = vir.shape[1]
    count = n_pair * tile_slots
    return pl.pallas_call(
        transform_kernel,
        out_shape=jax.ShapeDtypeStruct((n_occ * rows, columns, virtuals), jnp.bfloat16),
        grid_spec=pltpu.PrefetchScalarGridSpec(
            num_scalar_prefetch=2,
            grid=(n_occ,),
            in_specs=[
                pl.BlockSpec(
                    (1, n_pair, rows, tile_slots, width, width),
                    lambda o, *_: (o, 0, 0, 0, 0, 0),
                ),
                pl.BlockSpec((columns, total), lambda o, *_: (0, 0)),
                pl.BlockSpec((total, virtuals), lambda o, *_: (0, 0)),
            ],
            out_specs=pl.BlockSpec((rows, columns, virtuals), lambda o, *_: (o, 0, 0)),
            scratch_shapes=[
                pltpu.VMEM((rows * columns, total), jnp.float32),
                pltpu.VMEM((total, virtuals), jnp.bfloat16),
                pltpu.SMEM((count,), jnp.int32),
                pltpu.SMEM((count,), jnp.int32),
                pltpu.SMEM((total // width + 1,), jnp.int32),
                pltpu.SMEM((1,), jnp.int32),
            ],
        ),
        compiler_params=pltpu.CompilerParams(vmem_limit_bytes=56 * 2**20),
    )(slots, shell_size, integrals, panel, vir)


def send_integrals(
    mesh_shape,
    quarter_integrals,
    occ_coef,
    vir_coef,
    screened_block_mask,
    tile_holder_pair,
    shell_size,
):
    parts = mesh_shape["pair"] // mesh_shape["occ"]
    shard = occ_coef
    if parts > 1:
        wide = occ_coef.shape[1] // parts
        part = lax.rem(lax.axis_index("pair"), parts)
        shard = lax.dynamic_slice_in_dim(occ_coef, part * wide, wide, axis=1)
    gathered, panel, slots = gather(
        mesh_shape, shell_size, screened_block_mask, tile_holder_pair, quarter_integrals, shard
    )
    return transform(slots, shell_size, gathered, panel, vir_coef)


def pick_plan(mesh_shape):
    n_pair, n_occ = mesh_shape["pair"], mesh_shape["occ"]

    def per_device(quarter_integrals, occ_coef, vir_coef, *tables):
        rows, tile_slots, width, _ = quarter_integrals.shape
        columns = occ_coef.shape[1] * n_occ // n_pair
        integrals = n_occ * n_pair * quarter_integrals.size
        transformed = rows * columns * (
            n_pair * tile_slots * width + n_occ * occ_coef.shape[0]
        )
        if n_occ % 2 == 0 and n_pair % n_occ == 0 and integrals < transformed:
            plan = functools.partial(send_integrals, mesh_shape)
        else:
            plan = send_tiles
        return plan(quarter_integrals, occ_coef, vir_coef, *tables)

    return per_device


def solution(mesh):
    placed = (
        P(("frag", "occ"), "pair", None, None),
        P("frag", "occ"),
        P("frag", "occ"),
        P("frag", None),
        P("frag", None),
        P("frag"),
    )
    return jax.shard_map(
        pick_plan(dict(mesh.shape)), mesh=mesh, in_specs=placed, out_specs=P("frag", "pair", "occ"), check_vma=False
    )
```

```python
import functools

import jax
import jax.numpy as jnp
from jax import lax
from jax.experimental import pallas as pl
from jax.experimental.pallas import tpu as pltpu
from jax.sharding import PartitionSpec as P


def slot_lookup_table(screened_block_mask, tile_holder_pair, slot_count, tile_slots):
    block_count = screened_block_mask.shape[0]
    kept_tiles = screened_block_mask.reshape(-1)
    owners = tile_holder_pair.reshape(-1)
    tile_index = jnp.arange(kept_tiles.shape[0], dtype=jnp.int32)
    earlier = (
        (owners[:, None] == owners[None, :])
        & (tile_index[None, :] < tile_index[:, None])
        & (kept_tiles[None, :] == 1)
    )
    rank_within = jnp.sum(earlier.astype(jnp.int32), axis=1)
    slot_of = owners * tile_slots + rank_within
    slot_index = jnp.arange(slot_count, dtype=jnp.int32)
    holding = ((slot_of[None, :] == slot_index[:, None]) & (kept_tiles[None, :] == 1)).astype(
        jnp.int32
    )
    slot_occupied_flag = jnp.sum(holding, axis=1)
    slot_lambda_block = jnp.sum(holding * (tile_index // block_count)[None, :], axis=1)
    slot_sigma_block = jnp.sum(holding * (tile_index % block_count)[None, :], axis=1)
    return (slot_occupied_flag, slot_lambda_block, slot_sigma_block)


def trim_rows(coefficients, shell_size, slot_width):
    inside = jnp.arange(slot_width, dtype=jnp.int32)[None, :] < shell_size[:, None]
    return jnp.where(inside.reshape(-1)[:, None], coefficients, jnp.zeros((), coefficients.dtype))


def spread_tiles(placing, tile_parts):
    spread = jnp.einsum("kn,krjs->rjns", placing, tile_parts, preferred_element_type=jnp.float32)
    return spread.reshape(spread.shape[0], spread.shape[1], -1)


def send_tiles(
    quarter_integrals, occ_coef, vir_coef, screened_block_mask, tile_holder_pair, shell_size
):
    block_count = screened_block_mask.shape[0]
    slot_width = quarter_integrals.shape[3]
    tile_slots = quarter_integrals.shape[1]
    pair_count = lax.axis_size("pair")
    pair_index = lax.axis_index("pair")
    shard_width = occ_coef.shape[1]
    occ_total = shard_width * lax.axis_size("occ")
    slot_occupied_flag, slot_lambda_block, slot_sigma_block = slot_lookup_table(
        screened_block_mask, tile_holder_pair, pair_count * tile_slots, tile_slots
    )
    occ_used = trim_rows(occ_coef, shell_size, slot_width)
    vir_used = trim_rows(vir_coef, shell_size, slot_width)
    block_ids = jnp.arange(block_count, dtype=jnp.int32)
    placing = (
        (slot_sigma_block[:, None] == block_ids[None, :]) & (slot_occupied_flag[:, None] > 0)
    ).astype(jnp.bfloat16)
    own_lam = lax.dynamic_slice_in_dim(slot_lambda_block, pair_index * tile_slots, tile_slots)
    panel_whole = lax.all_gather(occ_used, "occ", axis=1, tiled=True)
    panel_rows = panel_whole.reshape(block_count, slot_width, occ_total)[own_lam]
    tile_parts = jnp.einsum(
        "rkls,klj->krjs", quarter_integrals, panel_rows, preferred_element_type=jnp.float32
    ).astype(jnp.bfloat16)
    summed = spread_tiles(
        placing, lax.all_to_all(tile_parts, "pair", split_axis=2, concat_axis=0, tiled=True)
    )
    half_mo = summed.astype(jnp.bfloat16)
    return jnp.einsum(
        "rjs,sb->rjb",
        lax.all_gather(half_mo, "occ", axis=0, tiled=True),
        vir_used,
        preferred_element_type=jnp.float32,
    ).astype(jnp.bfloat16)


MESH = pl.DeviceIdType.MESH


def gather_kernel(
    n_pair, n_occ, size_ref, mask_ref, owner_ref, integrals_ref, shard_ref,
    all_ref, turned_ref, slots_ref, panel_ref, local, z_send, z_recv, x_send, x_recv,
    core_send, core_recv, panel_send, panel_recv,
):
    cores = 2
    n_x = n_occ // cores
    z, occ = lax.axis_index("pair"), lax.axis_index("occ")
    x, core = occ // cores, lax.rem(occ, cores)
    sibling = x * cores + 1 - core
    holder = z // (n_pair // n_occ)
    holder_x, holder_core = holder // cores, lax.rem(holder, cores)
    z_peers = [lax.rem(z + d, n_pair) for d in range(1, n_pair)]
    x_peers = [lax.rem(x + d, n_x) for d in range(1, n_x)]

    barrier = pltpu.get_barrier_semaphore()
    for peer in z_peers:
        pl.semaphore_signal(barrier, inc=1, device_id={"pair": peer}, device_id_type=MESH)
    for peer in x_peers:
        pl.semaphore_signal(
            barrier, inc=1, device_id={"occ": peer * cores + core}, device_id_type=MESH
        )
    pl.semaphore_signal(barrier, inc=1, device_id={"occ": sibling}, device_id_type=MESH)
    pl.semaphore_wait(barrier, n_pair + n_x - 1)

    def along_z(d):
        return pltpu.make_async_remote_copy(
            src_ref=integrals_ref,
            dst_ref=all_ref.at[occ, z],
            send_sem=z_send.at[d],
            recv_sem=z_recv.at[d],
            device_id={"pair": lax.rem(z + d, n_pair)},
            device_id_type=MESH,
        )

    def block(x_of, d):
        return all_ref.at[x_of * cores + core, lax.rem(z + n_pair - d, n_pair)]

    def across_x(e, d):
        source = integrals_ref if d == 0 else block(x, d)
        return pltpu.make_async_remote_copy(
            src_ref=source,
            dst_ref=block(x, d),
            send_sem=x_send.at[e, d],
            recv_sem=x_recv.at[e, d],
            device_id={"occ": lax.rem(x + e, n_x) * cores + core},
            device_id_type=MESH,
        )

    def across_cores(e, d):
        x_of = lax.rem(x + n_x - e, n_x)
        source = integrals_ref if d == 0 and e == 0 else block(x_of, d)
        return pltpu.make_async_remote_copy(
            src_ref=source,
            dst_ref=block(x_of, d),
            send_sem=core_send.at[e, d],
            recv_sem=core_recv.at[e, d],
            device_id={"occ": sibling},
            device_id_type=MESH,
        )

    def panel_to(place, source, target):
        return pltpu.make_async_remote_copy(
            src_ref=source,
            dst_ref=panel_ref,
            send_sem=panel_send.at[place],
            recv_sem=panel_recv,
            device_id={"occ": target},
            device_id_type=MESH,
        )

    holds = occ == holder
    passes_on = jnp.logical_and(core == holder_core, x != holder_x)

    for d in range(1, n_pair):
        along_z(d).start()
    own = pltpu.make_async_copy(integrals_ref, all_ref.at[occ, z], local.at[0])
    own.start()
    own_panel = pltpu.make_async_copy(shard_ref, panel_ref, local.at[1])

    @pl.when(holds)
    def _():
        for e in range(1, n_x):
            panel_to(e, shard_ref, lax.rem(x + e, n_x) * cores + core).start()
        panel_to(0, shard_ref, sibling).start()
        own_panel.start()

    for e in range(1, n_x):
        across_x(e, 0).start()
    across_cores(0, 0).start()
    write_slots(n_pair, mask_ref, owner_ref, slots_ref)
    for d in range(1, n_pair):
        along_z(d).wait_recv()
        for e in range(1, n_x):
            across_x(e, d).start()
        across_cores(0, d).start()

    @pl.when(passes_on)
    def _():
        panel_to(0, panel_ref, sibling).wait_recv()
        panel_to(0, panel_ref, sibling).start()

    @pl.when(core != holder_core)
    def _():
        panel_to(0, panel_ref, sibling).wait_recv()

    @pl.when(holds)
    def _():
        own_panel.wait()

    turn_panel(size_ref, panel_ref, turned_ref)
    for d in range(n_pair):
        for e in range(1, n_x):
            across_x(e, d).wait_recv()
            across_cores(e, d).start()

    for e in range(n_x):
        for d in range(n_pair):
            across_cores(e, d).wait()
    for e in range(1, n_x):
        for d in range(n_pair):
            across_x(e, d).wait_send()
    for d in range(1, n_pair):
        along_z(d).wait_send()
    own.wait()

    @pl.when(holds)
    def _():
        for e in range(1, n_x):
            panel_to(e, shard_ref, sibling).wait_send()
        panel_to(0, shard_ref, sibling).wait_send()

    @pl.when(passes_on)
    def _():
        panel_to(0, panel_ref, sibling).wait_send()


def gather(mesh_shape, shell_size, mask, owner, integrals, shard):
    n_pair, n_occ = mesh_shape["pair"], mesh_shape["occ"]
    n_x = n_occ // 2
    slots = n_pair * integrals.shape[1]
    return pl.pallas_call(
        functools.partial(gather_kernel, n_pair, n_occ),
        out_shape=(
            jax.ShapeDtypeStruct((n_occ, n_pair) + integrals.shape, integrals.dtype),
            jax.ShapeDtypeStruct(shard.shape[::-1], shard.dtype),
            jax.ShapeDtypeStruct((3 * slots,), jnp.int32),
        ),
        in_specs=[
            pl.BlockSpec(memory_space=pltpu.SMEM),
            pl.BlockSpec(memory_space=pltpu.VMEM),
            pl.BlockSpec(memory_space=pltpu.VMEM),
            pl.BlockSpec(memory_space=pl.ANY),
            pl.BlockSpec(memory_space=pl.ANY),
        ],
        out_specs=(
            pl.BlockSpec(memory_space=pl.ANY),
            pl.BlockSpec(memory_space=pltpu.VMEM),
            pl.BlockSpec(memory_space=pltpu.SMEM),
        ),
        scratch_shapes=[
            pltpu.VMEM(shard.shape, shard.dtype),
            pltpu.SemaphoreType.DMA((2,)),
            pltpu.SemaphoreType.DMA((n_pair,)),
            pltpu.SemaphoreType.DMA((n_pair,)),
            pltpu.SemaphoreType.DMA((n_x, n_pair)),
            pltpu.SemaphoreType.DMA((n_x, n_pair)),
            pltpu.SemaphoreType.DMA((n_x, n_pair)),
            pltpu.SemaphoreType.DMA((n_x, n_pair)),
            pltpu.SemaphoreType.DMA((n_x,)),
            pltpu.SemaphoreType.DMA,
        ],
        compiler_params=pltpu.CompilerParams(
            collective_id=0, has_side_effects=True, vmem_limit_bytes=56 * 2**20
        ),
    )(shell_size, mask, owner, integrals, shard)


def write_slots(n_pair, mask_ref, owner_ref, slots_ref):
    shape = mask_ref.shape
    tile_slots = slots_ref.shape[0] // (3 * n_pair)
    row = lax.broadcasted_iota(jnp.int32, shape, 0)
    column = lax.broadcasted_iota(jnp.int32, shape, 1)
    before = (row < column).astype(jnp.float32)
    kept, owner = mask_ref[...] == 1, owner_ref[...]
    rows_of, columns_of = row.astype(jnp.float32), column.astype(jnp.float32)
    for p in range(n_pair):
        owned = (kept & (owner == p)).astype(jnp.float32)
        in_row = jnp.dot(owned, before, preferred_element_type=jnp.float32)
        sums = jnp.broadcast_to(jnp.sum(owned, axis=1, keepdims=True), shape)
        above = jnp.zeros(shape, jnp.float32)
        for i in range(shape[0]):
            above += jnp.where(row > i, sums[i : i + 1, :], 0.0)
        rank = in_row + above
        for k in range(tile_slots):
            chosen = jnp.where(rank == float(k), owned, 0.0)
            t = p * tile_slots + k
            slots_ref[3 * t] = jnp.sum(chosen).astype(jnp.int32)
            slots_ref[3 * t + 1] = jnp.sum(chosen * rows_of).astype(jnp.int32)
            slots_ref[3 * t + 2] = jnp.sum(chosen * columns_of).astype(jnp.int32)


def turn_panel(size_ref, panel_ref, turned_ref):
    total, columns = panel_ref.shape
    blocks = size_ref.shape[0]
    width = total // blocks
    place = lax.broadcasted_iota(jnp.int32, (width, columns), 0)
    for i in range(blocks):
        found = panel_ref[i * width : (i + 1) * width, :].astype(jnp.float32)
        used = jnp.where(place < size_ref[i], found, 0.0)
        turned_ref[:, i * width : (i + 1) * width] = used.T.astype(turned_ref.dtype)


def transform_kernel(
    slots_ref, size_ref, integrals_ref, panel_ref, vir_ref, out_ref,
    half_ref, kept_ref, rank_ref, first_ref, at_ref, count_ref,
):
    n_pair, rows, tile_slots, width, _ = integrals_ref.shape[1:]
    columns, total = panel_ref.shape
    blocks = total // width
    step = min(2 * width, total)

    @pl.when(pl.program_id(0) == 0)
    def _():
        count = jnp.int32(0)
        for t in range(n_pair * tile_slots):
            sig, rank, first = slots_ref[3 * t + 2], count, jnp.int32(1)
            for u in range(t):
                same = (slots_ref[3 * u] > 0) & (slots_ref[3 * u + 2] == sig)
                rank = jnp.where(same, rank_ref[u], rank)
                first = jnp.where(same, 0, first)
            rank_ref[t] = rank
            first_ref[t] = first
            at_ref[count] = sig
            count += first * slots_ref[3 * t]
        count_ref[0] = count
        half_ref[...] = jnp.zeros_like(half_ref)
        for i in range(blocks):

            @pl.when(i < count)
            def _():
                block = at_ref[i]
                shape = (width, vir_ref.shape[1])
                inside = lax.broadcasted_iota(jnp.int32, shape, 0) < size_ref[block]
                found = vir_ref[pl.ds(pl.multiple_of(block * width, width), width), :]
                kept_ref[i * width : (i + 1) * width, :] = jnp.where(
                    inside, found.astype(jnp.float32), 0.0
                ).astype(kept_ref.dtype)

            @pl.when(i >= count)
            def _():
                kept_ref[i * width : (i + 1) * width, :] = jnp.zeros(
                    (width, vir_ref.shape[1]), kept_ref.dtype
                )

    for p in range(n_pair):
        for k in range(tile_slots):
            t = p * tile_slots + k

            @pl.when(slots_ref[3 * t] > 0)
            def _():
                lam = pl.multiple_of(slots_ref[3 * t + 1] * width, width)
                place = pl.ds(pl.multiple_of(rank_ref[t] * width, width), width)
                tiles = jnp.concatenate([integrals_ref[0, p, r, k] for r in range(rows)], axis=1)
                part = jnp.dot(
                    panel_ref[:, pl.ds(lam, width)], tiles, preferred_element_type=jnp.float32
                )

                @pl.when(first_ref[t] > 0)
                def _():
                    for r in range(rows):
                        half_ref[r * columns : (r + 1) * columns, place] = part[
                            :, r * width : (r + 1) * width
                        ]

                @pl.when(first_ref[t] == 0)
                def _():
                    for r in range(rows):
                        half_ref[r * columns : (r + 1) * columns, place] += part[
                            :, r * width : (r + 1) * width
                        ]

    for n in range(1, -(-total // step) + 1):
        depth = min(n * step, total)

        @pl.when((count_ref[0] * width + step - 1) // step == n)
        def _():
            out_ref[...] = (
                jnp.dot(
                    half_ref[:, :depth].astype(jnp.bfloat16),
                    kept_ref[:depth, :],
                    preferred_element_type=jnp.float32,
                )
                .astype(out_ref.dtype)
                .reshape(out_ref.shape)
            )


def transform(slots, shell_size, integrals, panel, vir):
    n_occ, n_pair, rows, tile_slots, width, _ = integrals.shape
    columns, total = panel.shape
    virtuals = vir.shape[1]
    count = n_pair * tile_slots
    return pl.pallas_call(
        transform_kernel,
        out_shape=jax.ShapeDtypeStruct((n_occ * rows, columns, virtuals), jnp.bfloat16),
        grid_spec=pltpu.PrefetchScalarGridSpec(
            num_scalar_prefetch=2,
            grid=(n_occ,),
            in_specs=[
                pl.BlockSpec(
                    (1, n_pair, rows, tile_slots, width, width),
                    lambda o, *_: (o, 0, 0, 0, 0, 0),
                ),
                pl.BlockSpec((columns, total), lambda o, *_: (0, 0)),
                pl.BlockSpec((total, virtuals), lambda o, *_: (0, 0)),
            ],
            out_specs=pl.BlockSpec((rows, columns, virtuals), lambda o, *_: (o, 0, 0)),
            scratch_shapes=[
                pltpu.VMEM((rows * columns, total), jnp.float32),
                pltpu.VMEM((total, virtuals), jnp.bfloat16),
                pltpu.SMEM((count,), jnp.int32),
                pltpu.SMEM((count,), jnp.int32),
                pltpu.SMEM((total // width + 1,), jnp.int32),
                pltpu.SMEM((1,), jnp.int32),
            ],
        ),
        compiler_params=pltpu.CompilerParams(vmem_limit_bytes=56 * 2**20),
    )(slots, shell_size, integrals, panel, vir)


def send_integrals(
    mesh_shape,
    quarter_integrals,
    occ_coef,
    vir_coef,
    screened_block_mask,
    tile_holder_pair,
    shell_size,
):
    parts = mesh_shape["pair"] // mesh_shape["occ"]
    shard = occ_coef
    if parts > 1:
        wide = occ_coef.shape[1] // parts
        part = lax.rem(lax.axis_index("pair"), parts)
        shard = lax.dynamic_slice_in_dim(occ_coef, part * wide, wide, axis=1)
    gathered, panel, slots = gather(
        mesh_shape, shell_size, screened_block_mask, tile_holder_pair, quarter_integrals, shard
    )
    return transform(slots, shell_size, gathered, panel, vir_coef)


def pick_plan(mesh_shape):
    n_pair, n_occ = mesh_shape["pair"], mesh_shape["occ"]

    def per_device(quarter_integrals, occ_coef, vir_coef, *tables):
        rows, tile_slots, width, _ = quarter_integrals.shape
        columns = occ_coef.shape[1] * n_occ // n_pair
        integrals = n_occ * n_pair * quarter_integrals.size
        transformed = rows * columns * (
            n_pair * tile_slots * width + n_occ * occ_coef.shape[0]
        )
        if n_occ % 2 == 0 and n_pair % n_occ == 0 and integrals < transformed:
            plan = functools.partial(send_integrals, mesh_shape)
        else:
            plan = send_tiles
        return plan(quarter_integrals, occ_coef, vir_coef, *tables)

    return per_device


def solution(mesh):
    placed = (
        P(("frag", "occ"), "pair", None, None),
        P("frag", "occ"),
        P("frag", "occ"),
        P("frag", None),
        P("frag", None),
        P("frag"),
    )
    return jax.shard_map(
        pick_plan(dict(mesh.shape)), mesh=mesh, in_specs=placed, out_specs=P("frag", "pair", "occ"), check_vma=False
    )
```

```python
import functools

import jax
import jax.numpy as jnp
from jax import lax
from jax.experimental import pallas as pl
from jax.experimental.pallas import tpu as pltpu
from jax.sharding import PartitionSpec as P


def slot_lookup_table(screened_block_mask, tile_holder_pair, slot_count, tile_slots):
    block_count = screened_block_mask.shape[0]
    kept_tiles = screened_block_mask.reshape(-1)
    owners = tile_holder_pair.reshape(-1)
    tile_index = jnp.arange(kept_tiles.shape[0], dtype=jnp.int32)
    earlier = (
        (owners[:, None] == owners[None, :])
        & (tile_index[None, :] < tile_index[:, None])
        & (kept_tiles[None, :] == 1)
    )
    rank_within = jnp.sum(earlier.astype(jnp.int32), axis=1)
    slot_of = owners * tile_slots + rank_within
    slot_index = jnp.arange(slot_count, dtype=jnp.int32)
    holding = ((slot_of[None, :] == slot_index[:, None]) & (kept_tiles[None, :] == 1)).astype(
        jnp.int32
    )
    slot_occupied_flag = jnp.sum(holding, axis=1)
    slot_lambda_block = jnp.sum(holding * (tile_index // block_count)[None, :], axis=1)
    slot_sigma_block = jnp.sum(holding * (tile_index % block_count)[None, :], axis=1)
    return (slot_occupied_flag, slot_lambda_block, slot_sigma_block)


def trim_rows(coefficients, shell_size, slot_width):
    inside = jnp.arange(slot_width, dtype=jnp.int32)[None, :] < shell_size[:, None]
    return jnp.where(inside.reshape(-1)[:, None], coefficients, jnp.zeros((), coefficients.dtype))


def spread_tiles(placing, tile_parts):
    spread = jnp.einsum("kn,krjs->rjns", placing, tile_parts, preferred_element_type=jnp.float32)
    return spread.reshape(spread.shape[0], spread.shape[1], -1)


def send_tiles(
    quarter_integrals, occ_coef, vir_coef, screened_block_mask, tile_holder_pair, shell_size
):
    block_count = screened_block_mask.shape[0]
    slot_width = quarter_integrals.shape[3]
    tile_slots = quarter_integrals.shape[1]
    pair_count = lax.axis_size("pair")
    pair_index = lax.axis_index("pair")
    shard_width = occ_coef.shape[1]
    occ_total = shard_width * lax.axis_size("occ")
    slot_occupied_flag, slot_lambda_block, slot_sigma_block = slot_lookup_table(
        screened_block_mask, tile_holder_pair, pair_count * tile_slots, tile_slots
    )
    occ_used = trim_rows(occ_coef, shell_size, slot_width)
    vir_used = trim_rows(vir_coef, shell_size, slot_width)
    block_ids = jnp.arange(block_count, dtype=jnp.int32)
    placing = (
        (slot_sigma_block[:, None] == block_ids[None, :]) & (slot_occupied_flag[:, None] > 0)
    ).astype(jnp.bfloat16)
    own_lam = lax.dynamic_slice_in_dim(slot_lambda_block, pair_index * tile_slots, tile_slots)
    panel_whole = lax.all_gather(occ_used, "occ", axis=1, tiled=True)
    panel_rows = panel_whole.reshape(block_count, slot_width, occ_total)[own_lam]
    tile_parts = jnp.einsum(
        "rkls,klj->krjs", quarter_integrals, panel_rows, preferred_element_type=jnp.float32
    ).astype(jnp.bfloat16)
    summed = spread_tiles(
        placing, lax.all_to_all(tile_parts, "pair", split_axis=2, concat_axis=0, tiled=True)
    )
    half_mo = summed.astype(jnp.bfloat16)
    return jnp.einsum(
        "rjs,sb->rjb",
        lax.all_gather(half_mo, "occ", axis=0, tiled=True),
        vir_used,
        preferred_element_type=jnp.float32,
    ).astype(jnp.bfloat16)


MESH = pl.DeviceIdType.MESH


def gather_kernel(
    n_pair, n_occ, size_ref, mask_ref, owner_ref, integrals_ref, shard_ref,
    all_ref, turned_ref, slots_ref, panel_ref, local, z_send, z_recv, x_send, x_recv,
    core_send, core_recv, panel_send, panel_recv,
):
    cores = 2
    n_x = n_occ // cores
    z, occ = lax.axis_index("pair"), lax.axis_index("occ")
    x, core = occ // cores, lax.rem(occ, cores)
    sibling = x * cores + 1 - core
    holder = z // (n_pair // n_occ)
    holder_x, holder_core = holder // cores, lax.rem(holder, cores)
    z_peers = [lax.rem(z + d, n_pair) for d in range(1, n_pair)]
    x_peers = [lax.rem(x + d, n_x) for d in range(1, n_x)]

    barrier = pltpu.get_barrier_semaphore()
    for peer in z_peers:
        pl.semaphore_signal(barrier, inc=1, device_id={"pair": peer}, device_id_type=MESH)
    for peer in x_peers:
        pl.semaphore_signal(
            barrier, inc=1, device_id={"occ": peer * cores + core}, device_id_type=MESH
        )
    pl.semaphore_signal(barrier, inc=1, device_id={"occ": sibling}, device_id_type=MESH)
    pl.semaphore_wait(barrier, n_pair + n_x - 1)

    def along_z(d):
        return pltpu.make_async_remote_copy(
            src_ref=integrals_ref,
            dst_ref=all_ref.at[occ, z],
            send_sem=z_send.at[d],
            recv_sem=z_recv.at[d],
            device_id={"pair": lax.rem(z + d, n_pair)},
            device_id_type=MESH,
        )

    def block(x_of, d):
        return all_ref.at[x_of * cores + core, lax.rem(z + n_pair - d, n_pair)]

    def across_x(e, d):
        source = integrals_ref if d == 0 else block(x, d)
        return pltpu.make_async_remote_copy(
            src_ref=source,
            dst_ref=block(x, d),
            send_sem=x_send.at[e, d],
            recv_sem=x_recv.at[e, d],
            device_id={"occ": lax.rem(x + e, n_x) * cores + core},
            device_id_type=MESH,
        )

    def across_cores(e, d):
        x_of = lax.rem(x + n_x - e, n_x)
        source = integrals_ref if d == 0 and e == 0 else block(x_of, d)
        return pltpu.make_async_remote_copy(
            src_ref=source,
            dst_ref=block(x_of, d),
            send_sem=core_send.at[e, d],
            recv_sem=core_recv.at[e, d],
            device_id={"occ": sibling},
            device_id_type=MESH,
        )

    eased = n_x == 2 and n_pair == n_occ
    mate = z + 1 - 2 * lax.rem(z, 2)

    def crosses(d):
        of_mate = lax.rem(z + n_pair - d, n_pair) == mate
        return jnp.logical_not(jnp.logical_and(x == holder_x, of_mate))

    def when_crosses(d, act):
        if eased and d > 0:
            pl.when(crosses(d))(act)
        else:
            act()

    def relay():
        return pltpu.make_async_remote_copy(
            src_ref=block(1 - x, 0),
            dst_ref=block(1 - x, 0),
            send_sem=x_send.at[0, 0],
            recv_sem=x_recv.at[1, lax.rem(mate - z + n_pair, n_pair)],
            device_id={"pair": mate},
            device_id_type=MESH,
        )

    def panel_to(place, source, target):
        return pltpu.make_async_remote_copy(
            src_ref=source,
            dst_ref=panel_ref,
            send_sem=panel_send.at[place],
            recv_sem=panel_recv,
            device_id={"occ": target},
            device_id_type=MESH,
        )

    holds = occ == holder
    passes_on = jnp.logical_and(core == holder_core, x != holder_x)

    for d in range(1, n_pair):
        along_z(d).start()
    own = pltpu.make_async_copy(integrals_ref, all_ref.at[occ, z], local.at[0])
    own.start()
    own_panel = pltpu.make_async_copy(shard_ref, panel_ref, local.at[1])

    @pl.when(holds)
    def _():
        for e in range(1, n_x):
            panel_to(e, shard_ref, lax.rem(x + e, n_x) * cores + core).start()
        panel_to(0, shard_ref, sibling).start()
        own_panel.start()

    for e in range(1, n_x):
        across_x(e, 0).start()
    across_cores(0, 0).start()
    write_slots(n_pair, mask_ref, owner_ref, slots_ref)
    for d in range(1, n_pair):
        along_z(d).wait_recv()
        for e in range(1, n_x):
            when_crosses(d, lambda e=e, d=d: across_x(e, d).start())
        across_cores(0, d).start()

    for e in range(1, n_x):
        across_x(e, 0).wait_recv()
        across_cores(e, 0).start()

    if eased:

        @pl.when(x != holder_x)
        def _():
            relay().start()

    @pl.when(passes_on)
    def _():
        panel_to(0, panel_ref, sibling).wait_recv()
        panel_to(0, panel_ref, sibling).start()

    @pl.when(core != holder_core)
    def _():
        panel_to(0, panel_ref, sibling).wait_recv()

    @pl.when(holds)
    def _():
        own_panel.wait()

    turn_panel(size_ref, panel_ref, turned_ref)
    for d in range(1, n_pair):
        for e in range(1, n_x):
            across_x(e, d).wait_recv()
            across_cores(e, d).start()

    for e in range(n_x):
        for d in range(n_pair):
            across_cores(e, d).wait()
    for e in range(1, n_x):
        for d in range(n_pair):
            when_crosses(d, lambda e=e, d=d: across_x(e, d).wait_send())
    if eased:

        @pl.when(x != holder_x)
        def _():
            relay().wait_send()

    for d in range(1, n_pair):
        along_z(d).wait_send()
    own.wait()

    @pl.when(holds)
    def _():
        for e in range(1, n_x):
            panel_to(e, shard_ref, sibling).wait_send()
        panel_to(0, shard_ref, sibling).wait_send()

    @pl.when(passes_on)
    def _():
        panel_to(0, panel_ref, sibling).wait_send()


def gather(mesh_shape, shell_size, mask, owner, integrals, shard):
    n_pair, n_occ = mesh_shape["pair"], mesh_shape["occ"]
    n_x = n_occ // 2
    slots = n_pair * integrals.shape[1]
    return pl.pallas_call(
        functools.partial(gather_kernel, n_pair, n_occ),
        out_shape=(
            jax.ShapeDtypeStruct((n_occ, n_pair) + integrals.shape, integrals.dtype),
            jax.ShapeDtypeStruct(shard.shape[::-1], shard.dtype),
            jax.ShapeDtypeStruct((3 * slots,), jnp.int32),
        ),
        in_specs=[
            pl.BlockSpec(memory_space=pltpu.SMEM),
            pl.BlockSpec(memory_space=pltpu.VMEM),
            pl.BlockSpec(memory_space=pltpu.VMEM),
            pl.BlockSpec(memory_space=pl.ANY),
            pl.BlockSpec(memory_space=pl.ANY),
        ],
        out_specs=(
            pl.BlockSpec(memory_space=pl.ANY),
            pl.BlockSpec(memory_space=pltpu.VMEM),
            pl.BlockSpec(memory_space=pltpu.SMEM),
        ),
        scratch_shapes=[
            pltpu.VMEM(shard.shape, shard.dtype),
            pltpu.SemaphoreType.DMA((2,)),
            pltpu.SemaphoreType.DMA((n_pair,)),
            pltpu.SemaphoreType.DMA((n_pair,)),
            pltpu.SemaphoreType.DMA((n_x, n_pair)),
            pltpu.SemaphoreType.DMA((n_x, n_pair)),
            pltpu.SemaphoreType.DMA((n_x, n_pair)),
            pltpu.SemaphoreType.DMA((n_x, n_pair)),
            pltpu.SemaphoreType.DMA((n_x,)),
            pltpu.SemaphoreType.DMA,
        ],
        compiler_params=pltpu.CompilerParams(
            collective_id=0, has_side_effects=True, vmem_limit_bytes=56 * 2**20
        ),
    )(shell_size, mask, owner, integrals, shard)


def write_slots(n_pair, mask_ref, owner_ref, slots_ref):
    shape = mask_ref.shape
    tile_slots = slots_ref.shape[0] // (3 * n_pair)
    row = lax.broadcasted_iota(jnp.int32, shape, 0)
    column = lax.broadcasted_iota(jnp.int32, shape, 1)
    before = (row < column).astype(jnp.float32)
    kept, owner = mask_ref[...] == 1, owner_ref[...]
    rows_of, columns_of = row.astype(jnp.float32), column.astype(jnp.float32)
    for p in range(n_pair):
        owned = (kept & (owner == p)).astype(jnp.float32)
        in_row = jnp.dot(owned, before, preferred_element_type=jnp.float32)
        sums = jnp.broadcast_to(jnp.sum(owned, axis=1, keepdims=True), shape)
        above = jnp.zeros(shape, jnp.float32)
        for i in range(shape[0]):
            above += jnp.where(row > i, sums[i : i + 1, :], 0.0)
        rank = in_row + above
        for k in range(tile_slots):
            chosen = jnp.where(rank == float(k), owned, 0.0)
            t = p * tile_slots + k
            slots_ref[3 * t] = jnp.sum(chosen).astype(jnp.int32)
            slots_ref[3 * t + 1] = jnp.sum(chosen * rows_of).astype(jnp.int32)
            slots_ref[3 * t + 2] = jnp.sum(chosen * columns_of).astype(jnp.int32)


def turn_panel(size_ref, panel_ref, turned_ref):
    total, columns = panel_ref.shape
    blocks = size_ref.shape[0]
    width = total // blocks
    place = lax.broadcasted_iota(jnp.int32, (width, columns), 0)
    for i in range(blocks):
        found = panel_ref[i * width : (i + 1) * width, :].astype(jnp.float32)
        used = jnp.where(place < size_ref[i], found, 0.0)
        turned_ref[:, i * width : (i + 1) * width] = used.T.astype(turned_ref.dtype)


def transform_kernel(
    slots_ref, size_ref, integrals_ref, panel_ref, vir_ref, out_ref,
    half_ref, kept_ref, rank_ref, first_ref, at_ref, count_ref,
):
    n_pair, rows, tile_slots, width, _ = integrals_ref.shape[1:]
    columns, total = panel_ref.shape
    blocks = total // width
    step = min(2 * width, total)

    @pl.when(pl.program_id(0) == 0)
    def _():
        count = jnp.int32(0)
        for t in range(n_pair * tile_slots):
            sig, rank, first = slots_ref[3 * t + 2], count, jnp.int32(1)
            for u in range(t):
                same = (slots_ref[3 * u] > 0) & (slots_ref[3 * u + 2] == sig)
                rank = jnp.where(same, rank_ref[u], rank)
                first = jnp.where(same, 0, first)
            rank_ref[t] = rank
            first_ref[t] = first
            at_ref[count] = sig
            count += first * slots_ref[3 * t]
        count_ref[0] = count
        half_ref[...] = jnp.zeros_like(half_ref)
        for i in range(blocks):

            @pl.when(i < count)
            def _():
                block = at_ref[i]
                shape = (width, vir_ref.shape[1])
                inside = lax.broadcasted_iota(jnp.int32, shape, 0) < size_ref[block]
                found = vir_ref[pl.ds(pl.multiple_of(block * width, width), width), :]
                kept_ref[i * width : (i + 1) * width, :] = jnp.where(
                    inside, found.astype(jnp.float32), 0.0
                ).astype(kept_ref.dtype)

            @pl.when(i >= count)
            def _():
                kept_ref[i * width : (i + 1) * width, :] = jnp.zeros(
                    (width, vir_ref.shape[1]), kept_ref.dtype
                )

    for p in range(n_pair):
        for k in range(tile_slots):
            t = p * tile_slots + k

            @pl.when(slots_ref[3 * t] > 0)
            def _():
                lam = pl.multiple_of(slots_ref[3 * t + 1] * width, width)
                place = pl.ds(pl.multiple_of(rank_ref[t] * width, width), width)
                tiles = jnp.concatenate([integrals_ref[0, p, r, k] for r in range(rows)], axis=1)
                part = jnp.dot(
                    panel_ref[:, pl.ds(lam, width)], tiles, preferred_element_type=jnp.float32
                )

                @pl.when(first_ref[t] > 0)
                def _():
                    for r in range(rows):
                        half_ref[r * columns : (r + 1) * columns, place] = part[
                            :, r * width : (r + 1) * width
                        ]

                @pl.when(first_ref[t] == 0)
                def _():
                    for r in range(rows):
                        half_ref[r * columns : (r + 1) * columns, place] += part[
                            :, r * width : (r + 1) * width
                        ]

    for n in range(1, -(-total // step) + 1):
        depth = min(n * step, total)

        @pl.when((count_ref[0] * width + step - 1) // step == n)
        def _():
            out_ref[...] = (
                jnp.dot(
                    half_ref[:, :depth].astype(jnp.bfloat16),
                    kept_ref[:depth, :],
                    preferred_element_type=jnp.float32,
                )
                .astype(out_ref.dtype)
                .reshape(out_ref.shape)
            )


def transform(slots, shell_size, integrals, panel, vir):
    n_occ, n_pair, rows, tile_slots, width, _ = integrals.shape
    columns, total = panel.shape
    virtuals = vir.shape[1]
    count = n_pair * tile_slots
    return pl.pallas_call(
        transform_kernel,
        out_shape=jax.ShapeDtypeStruct((n_occ * rows, columns, virtuals), jnp.bfloat16),
        grid_spec=pltpu.PrefetchScalarGridSpec(
            num_scalar_prefetch=2,
            grid=(n_occ,),
            in_specs=[
                pl.BlockSpec(
                    (1, n_pair, rows, tile_slots, width, width),
                    lambda o, *_: (o, 0, 0, 0, 0, 0),
                ),
                pl.BlockSpec((columns, total), lambda o, *_: (0, 0)),
                pl.BlockSpec((total, virtuals), lambda o, *_: (0, 0)),
            ],
            out_specs=pl.BlockSpec((rows, columns, virtuals), lambda o, *_: (o, 0, 0)),
            scratch_shapes=[
                pltpu.VMEM((rows * columns, total), jnp.float32),
                pltpu.VMEM((total, virtuals), jnp.bfloat16),
                pltpu.SMEM((count,), jnp.int32),
                pltpu.SMEM((count,), jnp.int32),
                pltpu.SMEM((total // width + 1,), jnp.int32),
                pltpu.SMEM((1,), jnp.int32),
            ],
        ),
        compiler_params=pltpu.CompilerParams(vmem_limit_bytes=56 * 2**20),
    )(slots, shell_size, integrals, panel, vir)


def send_integrals(
    mesh_shape,
    quarter_integrals,
    occ_coef,
    vir_coef,
    screened_block_mask,
    tile_holder_pair,
    shell_size,
):
    parts = mesh_shape["pair"] // mesh_shape["occ"]
    shard = occ_coef
    if parts > 1:
        wide = occ_coef.shape[1] // parts
        part = lax.rem(lax.axis_index("pair"), parts)
        shard = lax.dynamic_slice_in_dim(occ_coef, part * wide, wide, axis=1)
    gathered, panel, slots = gather(
        mesh_shape, shell_size, screened_block_mask, tile_holder_pair, quarter_integrals, shard
    )
    return transform(slots, shell_size, gathered, panel, vir_coef)


def pick_plan(mesh_shape):
    n_pair, n_occ = mesh_shape["pair"], mesh_shape["occ"]

    def per_device(quarter_integrals, occ_coef, vir_coef, *tables):
        rows, tile_slots, width, _ = quarter_integrals.shape
        columns = occ_coef.shape[1] * n_occ // n_pair
        integrals = n_occ * n_pair * quarter_integrals.size
        transformed = rows * columns * (
            n_pair * tile_slots * width + n_occ * occ_coef.shape[0]
        )
        if n_occ % 2 == 0 and n_pair % n_occ == 0 and integrals < transformed:
            plan = functools.partial(send_integrals, mesh_shape)
        else:
            plan = send_tiles
        return plan(quarter_integrals, occ_coef, vir_coef, *tables)

    return per_device


def solution(mesh):
    placed = (
        P(("frag", "occ"), "pair", None, None),
        P("frag", "occ"),
        P("frag", "occ"),
        P("frag", None),
        P("frag", None),
        P("frag"),
    )
    return jax.shard_map(
        pick_plan(dict(mesh.shape)), mesh=mesh, in_specs=placed, out_specs=P("frag", "pair", "occ"), check_vma=False
    )
```

```python
import functools

import jax
import jax.numpy as jnp
from jax import lax
from jax.experimental import pallas as pl
from jax.experimental.pallas import tpu as pltpu
from jax.sharding import PartitionSpec as P


def slot_lookup_table(screened_block_mask, tile_holder_pair, slot_count, tile_slots):
    block_count = screened_block_mask.shape[0]
    kept_tiles = screened_block_mask.reshape(-1)
    owners = tile_holder_pair.reshape(-1)
    tile_index = jnp.arange(kept_tiles.shape[0], dtype=jnp.int32)
    earlier = (
        (owners[:, None] == owners[None, :])
        & (tile_index[None, :] < tile_index[:, None])
        & (kept_tiles[None, :] == 1)
    )
    rank_within = jnp.sum(earlier.astype(jnp.int32), axis=1)
    slot_of = owners * tile_slots + rank_within
    slot_index = jnp.arange(slot_count, dtype=jnp.int32)
    holding = ((slot_of[None, :] == slot_index[:, None]) & (kept_tiles[None, :] == 1)).astype(
        jnp.int32
    )
    slot_occupied_flag = jnp.sum(holding, axis=1)
    slot_lambda_block = jnp.sum(holding * (tile_index // block_count)[None, :], axis=1)
    slot_sigma_block = jnp.sum(holding * (tile_index % block_count)[None, :], axis=1)
    return (slot_occupied_flag, slot_lambda_block, slot_sigma_block)


def trim_rows(coefficients, shell_size, slot_width):
    inside = jnp.arange(slot_width, dtype=jnp.int32)[None, :] < shell_size[:, None]
    return jnp.where(inside.reshape(-1)[:, None], coefficients, jnp.zeros((), coefficients.dtype))


def spread_tiles(placing, tile_parts):
    spread = jnp.einsum("kn,krjs->rjns", placing, tile_parts, preferred_element_type=jnp.float32)
    return spread.reshape(spread.shape[0], spread.shape[1], -1)


def send_tiles(
    quarter_integrals, occ_coef, vir_coef, screened_block_mask, tile_holder_pair, shell_size
):
    block_count = screened_block_mask.shape[0]
    slot_width = quarter_integrals.shape[3]
    tile_slots = quarter_integrals.shape[1]
    pair_count = lax.axis_size("pair")
    pair_index = lax.axis_index("pair")
    shard_width = occ_coef.shape[1]
    occ_total = shard_width * lax.axis_size("occ")
    slot_occupied_flag, slot_lambda_block, slot_sigma_block = slot_lookup_table(
        screened_block_mask, tile_holder_pair, pair_count * tile_slots, tile_slots
    )
    occ_used = trim_rows(occ_coef, shell_size, slot_width)
    vir_used = trim_rows(vir_coef, shell_size, slot_width)
    block_ids = jnp.arange(block_count, dtype=jnp.int32)
    placing = (
        (slot_sigma_block[:, None] == block_ids[None, :]) & (slot_occupied_flag[:, None] > 0)
    ).astype(jnp.bfloat16)
    own_lam = lax.dynamic_slice_in_dim(slot_lambda_block, pair_index * tile_slots, tile_slots)
    panel_whole = lax.all_gather(occ_used, "occ", axis=1, tiled=True)
    panel_rows = panel_whole.reshape(block_count, slot_width, occ_total)[own_lam]
    tile_parts = jnp.einsum(
        "rkls,klj->krjs", quarter_integrals, panel_rows, preferred_element_type=jnp.float32
    ).astype(jnp.bfloat16)
    summed = spread_tiles(
        placing, lax.all_to_all(tile_parts, "pair", split_axis=2, concat_axis=0, tiled=True)
    )
    half_mo = summed.astype(jnp.bfloat16)
    return jnp.einsum(
        "rjs,sb->rjb",
        lax.all_gather(half_mo, "occ", axis=0, tiled=True),
        vir_used,
        preferred_element_type=jnp.float32,
    ).astype(jnp.bfloat16)


MESH = pl.DeviceIdType.MESH


def gather_kernel(
    n_pair, n_occ, size_ref, mask_ref, owner_ref, integrals_ref, shard_ref,
    all_ref, turned_ref, slots_ref, panel_ref, local, z_send, z_recv, x_send, x_recv,
    core_send, core_recv, panel_send, panel_recv,
):
    cores = 2
    n_x = n_occ // cores
    z, occ = lax.axis_index("pair"), lax.axis_index("occ")
    x, core = occ // cores, lax.rem(occ, cores)
    sibling = x * cores + 1 - core
    holder = z // (n_pair // n_occ)
    holder_x, holder_core = holder // cores, lax.rem(holder, cores)
    z_peers = [lax.rem(z + d, n_pair) for d in range(1, n_pair)]
    x_peers = [lax.rem(x + d, n_x) for d in range(1, n_x)]

    barrier = pltpu.get_barrier_semaphore()
    for peer in z_peers:
        pl.semaphore_signal(barrier, inc=1, device_id={"pair": peer}, device_id_type=MESH)
    for peer in x_peers:
        pl.semaphore_signal(
            barrier, inc=1, device_id={"occ": peer * cores + core}, device_id_type=MESH
        )
    pl.semaphore_signal(barrier, inc=1, device_id={"occ": sibling}, device_id_type=MESH)
    pl.semaphore_wait(barrier, n_pair + n_x - 1)

    def along_z(d):
        return pltpu.make_async_remote_copy(
            src_ref=integrals_ref,
            dst_ref=all_ref.at[occ, z],
            send_sem=z_send.at[d],
            recv_sem=z_recv.at[d],
            device_id={"pair": lax.rem(z + d, n_pair)},
            device_id_type=MESH,
        )

    def block(x_of, d):
        return all_ref.at[x_of * cores + core, lax.rem(z + n_pair - d, n_pair)]

    def across_x(e, d):
        source = integrals_ref if d == 0 else block(x, d)
        return pltpu.make_async_remote_copy(
            src_ref=source,
            dst_ref=block(x, d),
            send_sem=x_send.at[e, d],
            recv_sem=x_recv.at[e, d],
            device_id={"occ": lax.rem(x + e, n_x) * cores + core},
            device_id_type=MESH,
        )

    def across_cores(e, d):
        x_of = lax.rem(x + n_x - e, n_x)
        source = integrals_ref if d == 0 and e == 0 else block(x_of, d)
        return pltpu.make_async_remote_copy(
            src_ref=source,
            dst_ref=block(x_of, d),
            send_sem=core_send.at[e, d],
            recv_sem=core_recv.at[e, d],
            device_id={"occ": sibling},
            device_id_type=MESH,
        )

    def panel_to(place, source, target):
        return pltpu.make_async_remote_copy(
            src_ref=source,
            dst_ref=panel_ref,
            send_sem=panel_send.at[place],
            recv_sem=panel_recv,
            device_id={"occ": target},
            device_id_type=MESH,
        )

    holds = occ == holder
    passes_on = jnp.logical_and(core == holder_core, x != holder_x)

    for d in range(1, n_pair):
        along_z(d).start()
    own = pltpu.make_async_copy(integrals_ref, all_ref.at[occ, z], local.at[0])
    own.start()
    own_panel = pltpu.make_async_copy(shard_ref, panel_ref, local.at[1])

    @pl.when(holds)
    def _():
        for e in range(1, n_x):
            panel_to(e, shard_ref, lax.rem(x + e, n_x) * cores + core).start()
        panel_to(0, shard_ref, sibling).start()
        own_panel.start()

    for e in range(1, n_x):
        across_x(e, 0).start()
    across_cores(0, 0).start()
    write_slots(n_pair, mask_ref, owner_ref, slots_ref)
    for d in range(1, n_pair):
        along_z(d).wait_recv()
        for e in range(1, n_x):
            across_x(e, d).start()
        across_cores(0, d).start()

    @pl.when(passes_on)
    def _():
        panel_to(0, panel_ref, sibling).wait_recv()
        panel_to(0, panel_ref, sibling).start()

    @pl.when(core != holder_core)
    def _():
        panel_to(0, panel_ref, sibling).wait_recv()

    @pl.when(holds)
    def _():
        own_panel.wait()

    turn_panel(size_ref, panel_ref, turned_ref)
    for d in range(n_pair):
        for e in range(1, n_x):
            across_x(e, d).wait_recv()
            across_cores(e, d).start()

    for e in range(n_x):
        for d in range(n_pair):
            across_cores(e, d).wait()
    for e in range(1, n_x):
        for d in range(n_pair):
            across_x(e, d).wait_send()
    for d in range(1, n_pair):
        along_z(d).wait_send()
    own.wait()

    @pl.when(holds)
    def _():
        for e in range(1, n_x):
            panel_to(e, shard_ref, sibling).wait_send()
        panel_to(0, shard_ref, sibling).wait_send()

    @pl.when(passes_on)
    def _():
        panel_to(0, panel_ref, sibling).wait_send()


def gather(mesh_shape, shell_size, mask, owner, integrals, shard):
    n_pair, n_occ = mesh_shape["pair"], mesh_shape["occ"]
    n_x = n_occ // 2
    slots = n_pair * integrals.shape[1]
    return pl.pallas_call(
        functools.partial(gather_kernel, n_pair, n_occ),
        out_shape=(
            jax.ShapeDtypeStruct((n_occ, n_pair) + integrals.shape, integrals.dtype),
            jax.ShapeDtypeStruct(shard.shape[::-1], shard.dtype),
            jax.ShapeDtypeStruct((3 * slots,), jnp.int32),
        ),
        in_specs=[
            pl.BlockSpec(memory_space=pltpu.SMEM),
            pl.BlockSpec(memory_space=pltpu.VMEM),
            pl.BlockSpec(memory_space=pltpu.VMEM),
            pl.BlockSpec(memory_space=pl.ANY),
            pl.BlockSpec(memory_space=pl.ANY),
        ],
        out_specs=(
            pl.BlockSpec(memory_space=pl.ANY),
            pl.BlockSpec(memory_space=pltpu.VMEM),
            pl.BlockSpec(memory_space=pltpu.SMEM),
        ),
        scratch_shapes=[
            pltpu.VMEM(shard.shape, shard.dtype),
            pltpu.SemaphoreType.DMA((2,)),
            pltpu.SemaphoreType.DMA((n_pair,)),
            pltpu.SemaphoreType.DMA((n_pair,)),
            pltpu.SemaphoreType.DMA((n_x, n_pair)),
            pltpu.SemaphoreType.DMA((n_x, n_pair)),
            pltpu.SemaphoreType.DMA((n_x, n_pair)),
            pltpu.SemaphoreType.DMA((n_x, n_pair)),
            pltpu.SemaphoreType.DMA((n_x,)),
            pltpu.SemaphoreType.DMA,
        ],
        compiler_params=pltpu.CompilerParams(
            collective_id=0, has_side_effects=True, vmem_limit_bytes=56 * 2**20
        ),
    )(shell_size, mask, owner, integrals, shard)


def write_slots(n_pair, mask_ref, owner_ref, slots_ref):
    shape = mask_ref.shape
    tile_slots = slots_ref.shape[0] // (3 * n_pair)
    row = lax.broadcasted_iota(jnp.int32, shape, 0)
    column = lax.broadcasted_iota(jnp.int32, shape, 1)
    before = (row < column).astype(jnp.float32)
    kept, owner = mask_ref[...] == 1, owner_ref[...]
    rows_of, columns_of = row.astype(jnp.float32), column.astype(jnp.float32)
    for p in range(n_pair):
        owned = (kept & (owner == p)).astype(jnp.float32)
        in_row = jnp.dot(owned, before, preferred_element_type=jnp.float32)
        sums = jnp.broadcast_to(jnp.sum(owned, axis=1, keepdims=True), shape)
        above = jnp.zeros(shape, jnp.float32)
        for i in range(shape[0]):
            above += jnp.where(row > i, sums[i : i + 1, :], 0.0)
        rank = in_row + above
        for k in range(tile_slots):
            chosen = jnp.where(rank == float(k), owned, 0.0)
            t = p * tile_slots + k
            slots_ref[3 * t] = jnp.sum(chosen).astype(jnp.int32)
            slots_ref[3 * t + 1] = jnp.sum(chosen * rows_of).astype(jnp.int32)
            slots_ref[3 * t + 2] = jnp.sum(chosen * columns_of).astype(jnp.int32)


def turn_panel(size_ref, panel_ref, turned_ref):
    total, columns = panel_ref.shape
    blocks = size_ref.shape[0]
    width = total // blocks
    place = lax.broadcasted_iota(jnp.int32, (width, columns), 0)
    for i in range(blocks):
        found = panel_ref[i * width : (i + 1) * width, :].astype(jnp.float32)
        used = jnp.where(place < size_ref[i], found, 0.0)
        turned_ref[:, i * width : (i + 1) * width] = used.T.astype(turned_ref.dtype)


def transform_kernel(
    slots_ref, size_ref, integrals_ref, panel_ref, vir_ref, out_ref,
    half_ref, kept_ref, rank_ref, first_ref, at_ref, count_ref,
):
    n_pair, rows, tile_slots, width, _ = integrals_ref.shape[1:]
    columns, total = panel_ref.shape
    blocks = total // width
    step = min(2 * width, total)

    @pl.when(pl.program_id(0) == 0)
    def _():
        count = jnp.int32(0)
        for t in range(n_pair * tile_slots):
            sig, rank, first = slots_ref[3 * t + 2], count, jnp.int32(1)
            for u in range(t):
                same = (slots_ref[3 * u] > 0) & (slots_ref[3 * u + 2] == sig)
                rank = jnp.where(same, rank_ref[u], rank)
                first = jnp.where(same, 0, first)
            rank_ref[t] = rank
            first_ref[t] = first
            at_ref[count] = sig
            count += first * slots_ref[3 * t]
        count_ref[0] = count
        half_ref[...] = jnp.zeros_like(half_ref)
        for i in range(blocks):

            @pl.when(i < count)
            def _():
                block = at_ref[i]
                shape = (width, vir_ref.shape[1])
                inside = lax.broadcasted_iota(jnp.int32, shape, 0) < size_ref[block]
                found = vir_ref[pl.ds(pl.multiple_of(block * width, width), width), :]
                kept_ref[i * width : (i + 1) * width, :] = jnp.where(
                    inside, found.astype(jnp.float32), 0.0
                ).astype(kept_ref.dtype)

            @pl.when(i >= count)
            def _():
                kept_ref[i * width : (i + 1) * width, :] = jnp.zeros(
                    (width, vir_ref.shape[1]), kept_ref.dtype
                )

    for p in range(n_pair):
        for k in range(tile_slots):
            t = p * tile_slots + k

            @pl.when(slots_ref[3 * t] > 0)
            def _():
                lam = pl.multiple_of(slots_ref[3 * t + 1] * width, width)
                place = pl.ds(pl.multiple_of(rank_ref[t] * width, width), width)
                tiles = jnp.concatenate([integrals_ref[0, p, r, k] for r in range(rows)], axis=1)
                part = jnp.dot(
                    panel_ref[:, pl.ds(lam, width)], tiles, preferred_element_type=jnp.float32
                )

                @pl.when(first_ref[t] > 0)
                def _():
                    for r in range(rows):
                        half_ref[r * columns : (r + 1) * columns, place] = part[
                            :, r * width : (r + 1) * width
                        ]

                @pl.when(first_ref[t] == 0)
                def _():
                    for r in range(rows):
                        half_ref[r * columns : (r + 1) * columns, place] += part[
                            :, r * width : (r + 1) * width
                        ]

    for n in range(1, -(-total // step) + 1):
        depth = min(n * step, total)

        @pl.when((count_ref[0] * width + step - 1) // step == n)
        def _():
            for r in range(rows):
                out_ref[r] = jnp.dot(
                    half_ref[r * columns : (r + 1) * columns, :depth].astype(jnp.bfloat16),
                    kept_ref[:depth, :],
                    preferred_element_type=jnp.float32,
                ).astype(out_ref.dtype)


def transform(slots, shell_size, integrals, panel, vir):
    n_occ, n_pair, rows, tile_slots, width, _ = integrals.shape
    columns, total = panel.shape
    virtuals = vir.shape[1]
    count = n_pair * tile_slots
    return pl.pallas_call(
        transform_kernel,
        out_shape=jax.ShapeDtypeStruct((n_occ * rows, columns, virtuals), jnp.bfloat16),
        grid_spec=pltpu.PrefetchScalarGridSpec(
            num_scalar_prefetch=2,
            grid=(n_occ,),
            in_specs=[
                pl.BlockSpec(
                    (1, n_pair, rows, tile_slots, width, width),
                    lambda o, *_: (o, 0, 0, 0, 0, 0),
                ),
                pl.BlockSpec((columns, total), lambda o, *_: (0, 0)),
                pl.BlockSpec((total, virtuals), lambda o, *_: (0, 0)),
            ],
            out_specs=pl.BlockSpec((rows, columns, virtuals), lambda o, *_: (o, 0, 0)),
            scratch_shapes=[
                pltpu.VMEM((rows * columns, total), jnp.float32),
                pltpu.VMEM((total, virtuals), jnp.bfloat16),
                pltpu.SMEM((count,), jnp.int32),
                pltpu.SMEM((count,), jnp.int32),
                pltpu.SMEM((total // width + 1,), jnp.int32),
                pltpu.SMEM((1,), jnp.int32),
            ],
        ),
        compiler_params=pltpu.CompilerParams(vmem_limit_bytes=56 * 2**20),
    )(slots, shell_size, integrals, panel, vir)


def send_integrals(
    mesh_shape,
    quarter_integrals,
    occ_coef,
    vir_coef,
    screened_block_mask,
    tile_holder_pair,
    shell_size,
):
    parts = mesh_shape["pair"] // mesh_shape["occ"]
    shard = occ_coef
    if parts > 1:
        wide = occ_coef.shape[1] // parts
        part = lax.rem(lax.axis_index("pair"), parts)
        shard = lax.dynamic_slice_in_dim(occ_coef, part * wide, wide, axis=1)
    gathered, panel, slots = gather(
        mesh_shape, shell_size, screened_block_mask, tile_holder_pair, quarter_integrals, shard
    )
    return transform(slots, shell_size, gathered, panel, vir_coef)


def pick_plan(mesh_shape):
    n_pair, n_occ = mesh_shape["pair"], mesh_shape["occ"]

    def per_device(quarter_integrals, occ_coef, vir_coef, *tables):
        rows, tile_slots, width, _ = quarter_integrals.shape
        columns = occ_coef.shape[1] * n_occ // n_pair
        integrals = n_occ * n_pair * quarter_integrals.size
        transformed = rows * columns * (
            n_pair * tile_slots * width + n_occ * occ_coef.shape[0]
        )
        if n_occ % 2 == 0 and n_pair % n_occ == 0 and integrals < transformed:
            plan = functools.partial(send_integrals, mesh_shape)
        else:
            plan = send_tiles
        return plan(quarter_integrals, occ_coef, vir_coef, *tables)

    return per_device


def solution(mesh):
    placed = (
        P(("frag", "occ"), "pair", None, None),
        P("frag", "occ"),
        P("frag", "occ"),
        P("frag", None),
        P("frag", None),
        P("frag"),
    )
    return jax.shard_map(
        pick_plan(dict(mesh.shape)), mesh=mesh, in_specs=placed, out_specs=P("frag", "pair", "occ"), check_vma=False
    )
```
